256 devices in a mesh: tm: 64 (over z, x, core), det: 4 (over y).
Axes of the slice: x: 4, y: 4, z: 8, core: 2. Of those that a mesh axis runs over, the one named last changes fastest.
Arguments:
- strain: float32 [4, 65536], P('det', 'tm'), may hold values from -6 to 6
- decay_rate: float32 [8192], replicated, may hold values from 7.6293945e-07 to 0.0333333333
- frequency: float32 [8192], replicated, may hold values from 0.03 to 1.5
- gain: float32 [2, 8192], replicated, may hold values from -0.06455711 to 0.06455711
- member: int32 [8192], replicated, may hold values from 0 to 8191, each once
- sky_delay: int32 [64, 4], replicated, may hold values from 0 to 127
- antenna: float32 [64, 2, 4], replicated, may hold values from -2.1 to 2.1
Outputs:
- peak: float32 [32, 65536], P('det', 'tm')
The draws below stay inside these ranges and needn't reach their ends.
Inputs may be any that keep to these rules, and one draw needn't show every extreme that they name: `member`: a permutation of the 8192 pool filters.
All inputs are finite; a program needn't handle non-finite values.
Results may differ from the reference program's by a relative error of at most 0.0027.
Values sent between devices are 32-bit elements; how exact they have to be, the bound alone decides.
No kernel may reach another device: no remote copies, remote signals or barrier semaphores. Data moves between devices by JAX's collectives and lax.ppermute only.
A program may use at most 64 MiB of HBM per device.

```python
import math
import jax
import jax.numpy as jnp
from jax import lax

FILT = 256
TEMPL = 32
SKY = 64
DELAY = 128
NDET = 4
NT = 65536
NF = 8192


def rate_law(key, slow_share):
    pick_key, slow_key, fast_key = jax.random.split(key, 3)
    slow_mask = jax.random.uniform(pick_key, (NF,), jnp.float32) < slow_share
    slow_log = jax.random.uniform(slow_key, (NF,), jnp.float32, jnp.log(0.05 / NT), jnp.log(2.0 / NT))
    fast_log = jax.random.uniform(fast_key, (NF,), jnp.float32, jnp.log(2.0 / NT), jnp.log(1.0 / 30.0))
    rates = jnp.exp(jnp.where(slow_mask, slow_log, fast_log))
    return jnp.clip(rates, 0.05 / NT, 1.0 / 30.0)


def draw_decay_rate(key, part):
    slow_share = 0.5
    return rate_law(key, slow_share)


def draw_gain(key, part):
    slow_share = 0.5
    rates = rate_law(key, slow_share)
    key = jax.random.fold_in(key, 23)
    noise = jnp.clip(jax.random.normal(key, (2, NF), jnp.float32), -4.0, 4.0)
    spread = jnp.sqrt((2.0 * rates + 1.0 / NT) / FILT)
    return noise * spread[None, :]


def draw_sky_delay(key, part):
    key = jax.random.fold_in(key, 5)
    base_key, row_key, column_key, other_key = jax.random.split(key, 4)
    delays = jax.random.randint(base_key, (SKY, NDET), 0, DELAY, jnp.int32)
    row_pick = jax.random.randint(row_key, (), 0, SKY, jnp.int32)
    column_pick = jax.random.randint(column_key, (), 0, NDET, jnp.int32)
    other_pick = (column_pick + 1 + jax.random.randint(other_key, (), 0, NDET - 1, jnp.int32)) % NDET
    delays = delays.at[row_pick, column_pick].set(DELAY - 1)
    return delays.at[row_pick, other_pick].set(0)


def level_of(own_key, dims, pieces, least, top_value):
    def one(position, blocks):
        steps = jax.random.uniform(jax.random.fold_in(jax.random.fold_in(own_key, 6), position), (blocks,), jnp.float32, least / len(pieces), top_value / len(pieces))
        return jnp.repeat(jnp.exp(steps), dims[position] // blocks).reshape((-1,) + (1,) * (len(dims) - position - 1))

    level = one(*pieces[0])
    for cut in pieces[1:]:
        level = level * one(*cut)
    return level


def gaussian(key, dims, scale, bound, cuts=(), kind=jnp.bfloat16):
    values = scale * jax.random.normal(key, dims, jnp.float32)
    if cuts:
        values = values * level_of(key, dims, cuts, -0.22, 0.18)
    return jnp.clip(values, -bound, bound).astype(kind)


def setup_inputs(seed: int = 0) -> dict:
    key_list = jax.random.split(jax.random.key(seed), 8)
    strain = gaussian(key_list[0], (NDET, NT), 1.0, 6.0, ((0, 4), (1, 64)), jnp.float32)
    decay_rate = draw_decay_rate(jax.random.fold_in(key_list[7], 71), 0)
    frequency = jnp.clip(jax.random.uniform(key_list[2], (NF,), jnp.float32, 0.03, 1.5), 0.03, 1.5)
    gain = draw_gain(jax.random.fold_in(key_list[7], 71), 0)
    member = jax.random.permutation(key_list[4], NF).astype(jnp.int32)
    sky_delay = draw_sky_delay(jax.random.fold_in(key_list[7], 71), 0)
    antenna = gaussian(key_list[6], (SKY, 2, NDET), 0.35, 2.1, (), jnp.float32)
    return dict(strain=strain, decay_rate=decay_rate, frequency=frequency, gain=gain, member=member, sky_delay=sky_delay, antenna=antenna)


HIGHEST = lax.Precision.HIGHEST


def plain_powers(decay_rows, angle_rows, exponent_count):
    exponents = jnp.arange(exponent_count, dtype=jnp.float32)
    magnitude = jnp.exp(-decay_rows[..., None] * exponents)
    phase_angle = angle_rows[..., None] * exponents
    return magnitude * jnp.cos(phase_angle), magnitude * jnp.sin(phase_angle)


def local_filter(blocks, decay_rows, angle_rows, gain_real, gain_imag):
    block_width = blocks.shape[-1]
    power_real, power_imag = plain_powers(decay_rows, angle_rows, block_width + 1)
    scaled_real = gain_real[..., None] * power_real - gain_imag[..., None] * power_imag
    scaled_imag = gain_real[..., None] * power_imag + gain_imag[..., None] * power_real
    kernel_real = jnp.sum(scaled_real[..., :block_width], axis=1)
    kernel_imag = jnp.sum(scaled_imag[..., :block_width], axis=1)
    lag_matrix = jnp.arange(block_width)[:, None] - jnp.arange(block_width)[None, :]
    lag_index = jnp.clip(lag_matrix, 0, block_width - 1)
    causal = lag_matrix >= 0
    toeplitz_real = jnp.where(causal, kernel_real[:, lag_index], 0.0)
    toeplitz_imag = jnp.where(causal, kernel_imag[:, lag_index], 0.0)
    direct_real = jnp.einsum("gts,dms->gdmt", toeplitz_real, blocks, precision=HIGHEST)
    direct_imag = jnp.einsum("gts,dms->gdmt", toeplitz_imag, blocks, precision=HIGHEST)
    tail_real = scaled_real[..., block_width - 1::-1]
    tail_imag = scaled_imag[..., block_width - 1::-1]
    ends_real = jnp.einsum("gks,dms->gkdm", tail_real, blocks, precision=HIGHEST)
    ends_imag = jnp.einsum("gks,dms->gkdm", tail_imag, blocks, precision=HIGHEST)
    step_real = power_real[..., block_width][..., None]
    step_imag = power_imag[..., block_width][..., None]

    def advance(carried, element):
        state_real, state_imag = carried
        new_real = step_real * state_real - step_imag * state_imag + element[0]
        new_imag = step_real * state_imag + step_imag * state_real + element[1]
        return (new_real, new_imag), (state_real, state_imag)

    empty_state = jnp.zeros(ends_real.shape[:-1], jnp.float32)
    final_state, start_state = lax.scan(advance, (empty_state, empty_state),
                                        (jnp.moveaxis(ends_real, -1, 0), jnp.moveaxis(ends_imag, -1, 0)))
    lead_real = power_real[..., 1:]
    lead_imag = power_imag[..., 1:]
    output_real = direct_real + jnp.einsum("gkt,mgkd->gdmt", lead_real, start_state[0], precision=HIGHEST) \
        - jnp.einsum("gkt,mgkd->gdmt", lead_imag, start_state[1], precision=HIGHEST)
    output_imag = direct_imag + jnp.einsum("gkt,mgkd->gdmt", lead_real, start_state[1], precision=HIGHEST) \
        + jnp.einsum("gkt,mgkd->gdmt", lead_imag, start_state[0], precision=HIGHEST)
    shape_out = output_real.shape[:2] + (output_real.shape[2] * output_real.shape[3],)
    return output_real.reshape(shape_out), output_imag.reshape(shape_out)


def sky_peak(padded_real, padded_imag, sky_delay, antenna, length):
    detectors = padded_real.shape[1]

    def eight_skies(group_turn, running_max):
        for inner_sky in range(8):
            sky_index = group_turn * 8 + inner_sky
            totals = [jnp.zeros(running_max.shape, jnp.float32) for slot_index in range(4)]
            for detector in range(detectors):
                offset = sky_delay[sky_index, detector].astype(jnp.int32)
                piece_real = lax.dynamic_slice_in_dim(padded_real[:, detector], offset, length, 1)
                piece_imag = lax.dynamic_slice_in_dim(padded_imag[:, detector], offset, length, 1)
                for polarization in range(2):
                    weight = antenna[sky_index, polarization, detector]
                    totals[2 * polarization] = totals[2 * polarization] + weight * piece_real
                    totals[2 * polarization + 1] = totals[2 * polarization + 1] + weight * piece_imag
            energy = totals[0] * totals[0] + totals[1] * totals[1] + totals[2] * totals[2] + totals[3] * totals[3]
            running_max = jnp.maximum(running_max, energy)
        return running_max

    initial = jnp.zeros((padded_real.shape[0], length), jnp.float32)
    return lax.fori_loop(0, SKY // 8, eight_skies, initial)


def reference(strain, decay_rate, frequency, gain, member, sky_delay, antenna):
    block_width = math.gcd(128, NT)
    blocks = strain.reshape(NDET, NT // block_width, block_width)
    member_table = member.reshape(TEMPL // 8, 8, FILT)

    def one_group(member_rows):
        output_real, output_imag = local_filter(blocks, decay_rate[member_rows], frequency[member_rows],
                                                gain[0][member_rows], gain[1][member_rows])
        padding = jnp.zeros(output_real.shape[:-1] + (DELAY,), jnp.float32)
        padded_real = jnp.concatenate((output_real, padding), axis=-1)
        padded_imag = jnp.concatenate((output_imag, padding), axis=-1)
        return sky_peak(padded_real, padded_imag, sky_delay, antenna, NT)

    return lax.map(one_group, member_table).reshape(TEMPL, NT)
```

```python
import math

import jax
import jax.numpy as jnp
import numpy as np
from jax import lax
from jax.experimental import pallas as pl
from jax.experimental.pallas import tpu as pltpu
from jax.sharding import Mesh, PartitionSpec as P

FILT = 256
SKY = 64
WIDE = 8 * FILT
F32, BF16 = jnp.float32, jnp.bfloat16

TURN = 1.0 / (2.0 * math.pi)
TURN_HEAD = math.floor(TURN * 2**14) / 2**14
TURN_TAIL = TURN - TURN_HEAD

ROW_128, ROW_256, ROW_1024, ROW_8192 = 7, 8, 10, 13
ROW_GAIN, ROW_LEAD, ROWS = 16, 17, 24

VMEM_LIMIT = 56 * 2**20


def taylor(first, start, count):
    return [
        first * (-1) ** k * math.pi ** (2 * k + start) / math.factorial(2 * k + start)
        for k in range(count)
    ]


SINE, COSINE = taylor(1.0, 1, 8), taylor(1.0, 0, 9)


def horner(coefficients, square):
    total = jnp.full(square.shape, coefficients[-1], F32)
    for c in coefficients[-2::-1]:
        total = total * square + c
    return total


def cmul(ar, ai, br, bi):
    return ar * br - ai * bi, ar * bi + ai * br


def halves(x):
    head = x.astype(BF16)
    return head, (x - head.astype(F32)).astype(BF16)


def dot(a, b, contract_b=0):
    return lax.dot_general(
        a, b, (((1,), (contract_b,)), ((), ())), preferred_element_type=F32
    )


def dot3(a_head, a_tail, b_head, b_tail, contract_b=0):
    rows = a_head.shape[0]
    both = dot(jnp.concatenate([a_head, a_tail], axis=0), b_head, contract_b)
    return both[:rows] + both[rows:] + dot(a_head, b_tail, contract_b)


def prepare_kernel(
    place, strain, decay, frequency, gain, member, flip,
    sent, pr_head, pr_tail, pi_head, pi_tail, row_re, row_im, wr, wi, vr, vi,
    par,
):
    zi, xc, det = place[0], place[1], place[2]

    x = strain[...]
    head = x.astype(BF16)
    rest = x - head.astype(F32)
    middle = rest.astype(BF16)
    tail = (rest - middle.astype(F32)).astype(BF16)
    turned = dot(head, flip[...]) + (dot(middle, flip[...]) + dot(tail, flip[...]))
    for r in range(8):
        for p in range(32):
            sent[p, r : r + 1, :] = turned[7 - r : 8 - r, :]

    for half in range(2):
        index = member[pl.ds(pl.multiple_of(16 * det + 8 * half, 8), 8), :]
        high, low = index >> 7, index & 127

        def one_row(r, carried):
            hit = high == r
            values = (
                decay[pl.ds(r, 1), :],
                frequency[pl.ds(r, 1), :],
                gain[0, pl.ds(r, 1), :],
                gain[1, pl.ds(r, 1), :],
            )
            return tuple(
                jnp.where(
                    hit,
                    jnp.take_along_axis(jnp.broadcast_to(v, (8, 128)), low, axis=1),
                    c,
                )
                for v, c in zip(values, carried)
            )

        nothing = jnp.zeros((8, 128), F32)
        found = lax.fori_loop(0, 64, one_row, (nothing,) * 4, unroll=8)
        for k in range(4):
            par[k, 8 * half : 8 * half + 8, :] = found[k]

    power = jnp.left_shift(1, lax.broadcasted_iota(jnp.int32, (16, 128), 0)).astype(F32)
    place8 = lax.broadcasted_iota(jnp.int32, (8, 128), 0)
    ahead_z = zi - 1 - place8
    ahead_x = (xc + 7 - place8) & 7

    def choose(exponent, rows, re, im):
        out_re = jnp.ones((8, 128), F32)
        out_im = jnp.zeros((8, 128), F32)
        for bit, row in enumerate(rows):
            new_re, new_im = cmul(out_re, out_im, re[row : row + 1], im[row : row + 1])
            on = (exponent >> bit) & 1 == 1
            out_re = jnp.where(on, new_re, out_re)
            out_im = jnp.where(on, new_im, out_im)
        return out_re, out_im

    def one_chunk(c, _):
        lanes = pl.ds(pl.multiple_of(c * 128, 128), 128)
        f = par[1, pl.ds(c, 1), :]
        f_head = jnp.floor(f * 2048.0) * (1.0 / 2048.0)
        f_tail = f - f_head
        first = power * (f_head * TURN_HEAD)
        second = power * (f_head * TURN_TAIL + f_tail * TURN)
        turn = (first - jnp.floor(first + 0.5)) + (second - jnp.floor(second + 0.5))
        turn = turn - jnp.floor(turn + 0.5)
        square = turn * turn
        sine = turn * horner(SINE, square)
        cosine = horner(COSINE, square)
        size = jnp.exp(-power * par[0, pl.ds(c, 1), :])
        re = size * (1.0 - 2.0 * sine * sine)
        im = size * (2.0 * sine * cosine)
        row_re[0:16, lanes] = re
        row_im[0:16, lanes] = im
        g_re, g_im = par[2, pl.ds(c, 1), :], par[3, pl.ds(c, 1), :]
        l_re, l_im = cmul(g_re, g_im, re[0:1], im[0:1])
        empty = jnp.zeros((6, 128), F32)
        row_re[16:24, lanes] = jnp.concatenate([g_re, l_re, empty], axis=0)
        row_im[16:24, lanes] = jnp.concatenate([g_im, l_im, empty], axis=0)
        w_re, w_im = choose(ahead_z, (13, 14, 15), re, im)
        wr[:, lanes] = jnp.where(ahead_z >= 0, w_re, 0.0)
        wi[:, lanes] = jnp.where(ahead_z >= 0, w_im, 0.0)
        vr[:, lanes], vi[:, lanes] = choose(ahead_x, (10, 11, 12), re, im)
        t_re, t_im = choose(place8, (0, 1, 2), re, im)
        for row in range(3, 8):
            n_re, n_im = cmul(t_re, t_im, re[row : row + 1], im[row : row + 1])
            t_re = jnp.concatenate([t_re, n_re], axis=0)
            t_im = jnp.concatenate([t_im, n_im], axis=0)
        pr_head[:, lanes], pr_tail[:, lanes] = halves(t_re)
        pi_head[:, lanes], pi_tail[:, lanes] = halves(t_im)
        return 0

    lax.fori_loop(0, WIDE // 128, one_chunk, 0)


def column_kernel(
    place, x, pr_head, pr_tail, pi_head, pi_tail, row_re, row_im, wr, wi,
    sent, lhs_head, lhs_tail,
):
    zi, xc = place[0], place[1]
    for q in range(4):
        rows = jnp.concatenate(
            [x[pl.ds(2 * q, 32, stride=8), :], x[pl.ds(2 * q + 1, 32, stride=8), :]],
            axis=1,
        )
        lhs_head[32 * q : 32 * q + 32, :], lhs_tail[32 * q : 32 * q + 32, :] = halves(rows)
    own = lax.broadcasted_iota(jnp.int32, (8, 256), 0) == zi

    def one_part(part, _):
        lanes = pl.ds(pl.multiple_of(part * 256, 256), 256)
        a_head, a_tail = lhs_head[...], lhs_tail[...]
        e_re = dot3(a_head, a_tail, pr_head[:, lanes], pr_tail[:, lanes])
        e_im = dot3(a_head, a_tail, pi_head[:, lanes], pi_tail[:, lanes])
        step_re = row_re[ROW_256 : ROW_256 + 1, lanes]
        step_im = row_im[ROW_256 : ROW_256 + 1, lanes]
        s_re, s_im = e_re[96:128], e_im[96:128]
        for q in (2, 1, 0):
            s_re, s_im = cmul(s_re, s_im, step_re, step_im)
            s_re = s_re + e_re[32 * q : 32 * q + 32]
            s_im = s_im + e_im[32 * q : 32 * q + 32]
        w_re, w_im = wr[:, lanes], wi[:, lanes]
        before_re, before_im, own_re, own_im = [], [], [], []
        for d in range(4):
            d_re, d_im = s_re[8 * d : 8 * d + 8], s_im[8 * d : 8 * d + 8]
            t_re, t_im = cmul(d_re, d_im, w_re, w_im)
            before_re.append(jnp.sum(t_re, axis=0, keepdims=True))
            before_im.append(jnp.sum(t_im, axis=0, keepdims=True))
            own_re.append(jnp.sum(jnp.where(own, d_re, 0.0), axis=0, keepdims=True))
            own_im.append(jnp.sum(jnp.where(own, d_im, 0.0), axis=0, keepdims=True))
        b_re, b_im, o_re, o_im = (
            jnp.concatenate(v, axis=0) for v in (before_re, before_im, own_re, own_im)
        )
        i_re, i_im = cmul(
            b_re, b_im,
            row_re[ROW_8192 : ROW_8192 + 1, lanes], row_im[ROW_8192 : ROW_8192 + 1, lanes],
        )
        without = jnp.concatenate([b_re, b_im], axis=0)
        within = jnp.concatenate([i_re + o_re, i_im + o_im], axis=0)
        for p in range(8):
            sent[p, :, lanes] = jnp.where(xc < p, within, without)
        return 0

    lax.fori_loop(0, WIDE // 256, one_part, 0)

    shard = jnp.where(xc == 0, zi + 1, zi)
    inside = shard < 8
    row = jnp.minimum(shard, 7) * 8 + 7
    halo = jnp.concatenate(
        [x[pl.ds(row + 64 * d, 1), :] for d in range(4)] + [jnp.zeros((4, 128), F32)],
        axis=0,
    )
    halo = jnp.where(inside, halo, 0.0)
    for p in range(8):
        sent[p, :, WIDE : WIDE + 128] = halo


def peak_kernel(
    place, delay, antenna, got, x, pr_head, pr_tail, pi_head, pi_tail, row_re, row_im, vr, vi, flip,
    out, blocks, e_re, e_im, s_re, s_im, snr, grouped, shifted,
):
    zi, xc = place[0], place[1]
    last = jnp.logical_and(zi == 7, xc == 7)

    for m in range(8):
        for d in range(4):
            blocks[4 * m + d : 4 * m + d + 1, :] = x[
                pl.ds(64 * d + 8 * zi + (7 - m), 1), :
            ]
    blocks[32:40, :] = got[(xc + 1) & 7, :, WIDE : WIDE + 128]
    x_head, x_tail = halves(blocks[...])
    n_head, n_tail = (dot(v, flip[...]).astype(BF16) for v in (x_head, x_tail))

    def one_part(part, _):
        lanes = pl.ds(pl.multiple_of(part * 256, 256), 256)
        a_head, a_tail = x_head[0:32], x_tail[0:32]
        l_re = dot3(a_head, a_tail, pr_head[0:128, lanes], pr_tail[0:128, lanes])
        l_im = dot3(a_head, a_tail, pi_head[0:128, lanes], pi_tail[0:128, lanes])
        q_re = jnp.zeros((4, 256), F32)
        q_im = jnp.zeros((4, 256), F32)
        for p in range(8):
            t_re, t_im = cmul(
                got[p, 0:4, lanes], got[p, 4:8, lanes],
                vr[p : p + 1, lanes], vi[p : p + 1, lanes],
            )
            q_re, q_im = q_re + t_re, q_im + t_im
        step_re = row_re[ROW_128 : ROW_128 + 1, lanes]
        step_im = row_im[ROW_128 : ROW_128 + 1, lanes]
        g_re = row_re[ROW_LEAD : ROW_LEAD + 1, lanes]
        g_im = row_im[ROW_LEAD : ROW_LEAD + 1, lanes]
        for m in range(9):
            t_re, t_im = cmul(q_re, q_im, g_re, g_im)
            if m == 8:
                t_re = jnp.where(last, 0.0, t_re)
                t_im = jnp.where(last, 0.0, t_im)
            s_re[4 * m : 4 * m + 4, lanes] = t_re
            s_im[4 * m : 4 * m + 4, lanes] = t_im
            if m < 8:
                q_re, q_im = cmul(q_re, q_im, step_re, step_im)
                q_re = q_re + l_re[4 * m : 4 * m + 4]
                q_im = q_im + l_im[4 * m : 4 * m + 4]
        s_re[36:40, lanes] = jnp.broadcast_to(row_re[ROW_GAIN : ROW_GAIN + 1, lanes], (4, 256))
        s_im[36:40, lanes] = jnp.broadcast_to(row_im[ROW_GAIN : ROW_GAIN + 1, lanes], (4, 256))

        both_head, both_tail = halves(jnp.concatenate([s_re[:, lanes], s_im[:, lanes]], axis=0))
        lead_head = jnp.concatenate([pr_head[0:128, lanes], pi_head[0:128, lanes]], axis=0)
        lead_tail = jnp.concatenate([pr_tail[0:128, lanes], pi_tail[0:128, lanes]], axis=0)
        full = dot3(both_head, both_tail, lead_head, lead_tail, 1)
        f_re = full[0:40, 0:128] - full[40:80, 128:256]
        f_im = full[0:40, 128:256] + full[40:80, 0:128]
        lag = lax.broadcasted_iota(jnp.int32, (128, 128), 1) - lax.broadcasted_iota(
            jnp.int32, (128, 128), 0
        )
        response = []
        for f in (f_re, f_im):
            spread = jnp.broadcast_to(f[36:37, :], (128, 128))
            rolled = pltpu.roll(spread, 0, 1, stride=1, stride_axis=0)
            response.append(jnp.where(lag >= 0, rolled, 0.0))
        r_head, r_tail = halves(jnp.concatenate(response, axis=1))
        direct = dot3(n_head, n_tail, r_head, r_tail)
        snr[0] = f_re + direct[:, 0:128]
        snr[1] = f_im + direct[:, 128:256]
        for c in range(2):
            for d in range(4):
                grouped[c, d, pl.ds(part, 9, stride=8), :] = snr[c, pl.ds(d, 9, stride=4), :]
        return 0

    grouped[:, :, 72:128, :] = jnp.zeros((2, 4, 56, 128), F32)
    lax.fori_loop(0, WIDE // 256, one_part, 0)

    early = lax.broadcasted_iota(jnp.int32, (64, 128), 1) < 64
    for c in range(2):
        for d in range(4):
            t = grouped[c, d].T
            top, low = t[0:64], t[64:128]
            ahead_top, ahead_low = pltpu.roll(top, 120, 1), pltpu.roll(low, 120, 1)
            shifted[c, d, 0:64, :] = jnp.where(early, top, pltpu.roll(low, 64, 1))
            shifted[c, d, 64:128, :] = jnp.where(early, low, pltpu.roll(top, 56, 1))
            shifted[c, d, 128:192, :] = jnp.where(early, ahead_top, pltpu.roll(low, 56, 1))

    def one_sky(s, best):
        total = [None] * 4
        for d in range(4):
            rows = pl.ds(delay[4 * s + d], 64)
            for c in range(2):
                piece = shifted[c, d, rows, :]
                for p in range(2):
                    term = antenna[8 * s + 4 * p + d] * piece
                    k = 2 * p + c
                    total[k] = term if total[k] is None else total[k] + term
        energy = (total[0] * total[0] + total[1] * total[1]) + (
            total[2] * total[2] + total[3] * total[3]
        )
        return jnp.maximum(best, energy)

    best = lax.fori_loop(0, SKY, one_sky, jnp.zeros((64, 128), F32), unroll=2)
    turned = best.T
    for m in range(8):
        out[:, 128 * m : 128 * m + 128] = jnp.concatenate(
            [turned[8 * m : 8 * m + 8], turned[64 + 8 * m : 72 + 8 * m]], axis=1
        )


def call(kernel, n_scalar, n_vector, shapes, scratch):
    scalar, vector = (pl.BlockSpec(memory_space=m) for m in (pltpu.SMEM, pltpu.VMEM))
    return pl.pallas_call(
        kernel,
        out_shape=[jax.ShapeDtypeStruct(*s) for s in shapes],
        in_specs=[scalar] * n_scalar + [vector] * n_vector,
        out_specs=[vector] * len(shapes),
        scratch_shapes=[pltpu.VMEM(*s) for s in scratch],
        compiler_params=pltpu.CompilerParams(vmem_limit_bytes=VMEM_LIMIT),
    )


def shards(strain, decay_rate, frequency, gain, member, sky_delay, antenna):
    plane = 2 * lax.axis_index("x") + lax.axis_index("core")
    place = jnp.stack([lax.axis_index("z"), plane, lax.axis_index("det")]).astype(jnp.int32)
    flip = jnp.asarray(np.eye(128, dtype=np.float32)[::-1], dtype=BF16)
    table = ((256, WIDE), BF16)
    rows = ((ROWS, WIDE), F32)
    eight = ((8, WIDE), F32)
    sent, prh, prt, pih, pit, rr, ri, wr, wi, vr, vi = call(
        prepare_kernel, 1, 6,
        [((32, 8, 128), F32), table, table, table, table, rows, rows, eight, eight, eight, eight],
        [((4, 16, 128), F32)],
    )(
        place, strain.reshape(8, 128), decay_rate.reshape(64, 128), frequency.reshape(64, 128),
        gain.reshape(2, 64, 128), member.reshape(64, 128), flip,
    )
    column = lax.all_to_all(sent, ("det", "z"), 0, 0, tiled=True).reshape(256, 128)
    (partial,) = call(
        column_kernel, 1, 9, [((8, 8, WIDE + 128), F32)], [((128, 256), BF16), ((128, 256), BF16)]
    )(place, column, prh, prt, pih, pit, rr, ri, wr, wi)
    got = lax.all_to_all(partial, ("x", "core"), 0, 0, tiled=True)
    (peak,) = call(
        peak_kernel, 3, 11, [((8, 1024), F32)],
        [
            ((40, 128), F32), ((32, WIDE), F32), ((32, WIDE), F32), ((40, WIDE), F32),
            ((40, WIDE), F32), ((2, 40, 128), F32), ((2, 4, 128, 128), F32),
            ((2, 4, 192, 128), F32),
        ],
    )(
        place, sky_delay.reshape(-1), antenna.reshape(-1),
        got, column, prh, prt, pih, pit, rr, ri, vr, vi, flip,
    )
    return peak


def solution(mesh):
    fine = Mesh(mesh.devices.reshape(8, 4, 2, 4), ("z", "x", "core", "det"))
    time = ("z", "x", "core")
    in_specs = (P("det", time), P(), P(), P(), P(), P(), P())
    return jax.shard_map(
        shards, mesh=fine, in_specs=in_specs, out_specs=P("det", time), check_vma=False
    )
```

```python
import math

import jax
import jax.numpy as jnp
import numpy as np
from jax import lax
from jax.experimental import pallas as pl
from jax.experimental.pallas import tpu as pltpu
from jax.sharding import Mesh, PartitionSpec as P

FILT = 256
SKY = 64
WIDE = 8 * FILT
F32, BF16 = jnp.float32, jnp.bfloat16

TURN = 1.0 / (2.0 * math.pi)
TURN_HEAD = math.floor(TURN * 2**14) / 2**14
TURN_TAIL = TURN - TURN_HEAD

ROW_128, ROW_8192, ROW_GAIN, ROW_LEAD = 0, 1, 2, 3

VMEM_LIMIT = 16 * 2**20
UNROLL = True


def taylor(first, start, count):
    return [
        first * (-1) ** k * math.pi ** (2 * k + start) / math.factorial(2 * k + start)
        for k in range(count)
    ]


SINE, COSINE = taylor(1.0, 1, 8), taylor(1.0, 0, 9)


def horner(coefficients, square):
    total = jnp.full(square.shape, coefficients[-1], F32)
    for c in coefficients[-2::-1]:
        total = total * square + c
    return total


def cmul(ar, ai, br, bi):
    return ar * br - ai * bi, ar * bi + ai * br


def halves(x):
    head = x.astype(BF16)
    return head, (x - head.astype(F32)).astype(BF16)


def dot(a, b, contract_b=0):
    return lax.dot_general(
        a, b, (((1,), (contract_b,)), ((), ())), preferred_element_type=F32
    )


def dot3(a_head, a_tail, b_head, b_tail, contract_b=0):
    rows = a_head.shape[0]
    both = dot(jnp.concatenate([a_head, a_tail], axis=0), b_head, contract_b)
    return both[:rows] + both[rows:] + dot(a_head, b_tail, contract_b)


def lead_tables(lanes, pr_head, pr_tail, pi_head, pi_tail):
    return (
        jnp.concatenate([pr_head[:, lanes], pi_head[:, lanes]], axis=0),
        jnp.concatenate([pr_tail[:, lanes], pi_tail[:, lanes]], axis=0),
    )


def prepare_kernel(
    place, decay, frequency, gain, member,
    pr_head, pr_tail, pi_head, pi_tail, row_re, row_im, wr, wi, vr, vi, response,
    par,
):
    zi, xc, det = place[0], place[1], place[2]

    index = [
        member[pl.ds(pl.multiple_of(16 * det + 8 * half, 8), 8), :] for half in range(2)
    ]
    high, low = [v >> 7 for v in index], [v & 127 for v in index]

    def one_row(r, carried):
        lanes = pl.ds(pl.multiple_of(r * 128, 128), 128)
        values = (
            decay[pl.ds(r, 1), :],
            frequency[pl.ds(r, 1), :],
            gain[0:1, lanes],
            gain[1:2, lanes],
        )
        spread = [jnp.broadcast_to(v, (8, 128)) for v in values]
        return tuple(
            jnp.where(
                high[h] == r,
                jnp.take_along_axis(spread[k], low[h], axis=1),
                carried[4 * h + k],
            )
            for h in range(2)
            for k in range(4)
        )

    nothing = jnp.zeros((8, 128), F32)
    found = lax.fori_loop(0, 64, one_row, (nothing,) * 8, unroll=8)
    for h in range(2):
        for k in range(4):
            par[k, 8 * h : 8 * h + 8, :] = found[4 * h + k]

    power = jnp.left_shift(1, lax.broadcasted_iota(jnp.int32, (16, 128), 0)).astype(F32)
    place8 = lax.broadcasted_iota(jnp.int32, (8, 128), 0)
    ahead_z = zi - 1 - place8
    ahead_x = (place8 + 7 - xc) & 7

    def choose(exponent, rows, re, im):
        out_re = jnp.ones((8, 128), F32)
        out_im = jnp.zeros((8, 128), F32)
        for bit, row in enumerate(rows):
            new_re, new_im = cmul(out_re, out_im, re[row : row + 1], im[row : row + 1])
            on = (exponent >> bit) & 1 == 1
            out_re = jnp.where(on, new_re, out_re)
            out_im = jnp.where(on, new_im, out_im)
        return out_re, out_im

    def one_chunk(c, _):
        lanes = pl.ds(pl.multiple_of(c * 128, 128), 128)
        f = par[1, pl.ds(c, 1), :]
        f_head = jnp.floor(f * 2048.0) * (1.0 / 2048.0)
        f_tail = f - f_head
        first = power * (f_head * TURN_HEAD)
        second = power * (f_head * TURN_TAIL + f_tail * TURN)
        turn = (first - jnp.floor(first + 0.5)) + (second - jnp.floor(second + 0.5))
        turn = turn - jnp.floor(turn + 0.5)
        square = turn * turn
        sine = turn * horner(SINE, square)
        cosine = horner(COSINE, square)
        size = jnp.exp(-power * par[0, pl.ds(c, 1), :])
        re = size * (1.0 - 2.0 * sine * sine)
        im = size * (2.0 * sine * cosine)
        g_re, g_im = par[2, pl.ds(c, 1), :], par[3, pl.ds(c, 1), :]
        l_re, l_im = cmul(g_re, g_im, re[0:1], im[0:1])
        empty = jnp.zeros((4, 128), F32)
        row_re[:, lanes] = jnp.concatenate([re[7:8], re[13:14], g_re, l_re, empty], axis=0)
        row_im[:, lanes] = jnp.concatenate([im[7:8], im[13:14], g_im, l_im, empty], axis=0)
        w_re, w_im = choose(ahead_z, (13, 14, 15), re, im)
        wr[:, lanes] = jnp.where(ahead_z >= 0, w_re, 0.0)
        wi[:, lanes] = jnp.where(ahead_z >= 0, w_im, 0.0)
        vr[:, lanes], vi[:, lanes] = choose(ahead_x, (10, 11, 12), re, im)
        t_re, t_im = choose(place8, (0, 1, 2), re, im)
        for row in range(3, 7):
            n_re, n_im = cmul(t_re, t_im, re[row : row + 1], im[row : row + 1])
            t_re = jnp.concatenate([t_re, n_re], axis=0)
            t_im = jnp.concatenate([t_im, n_im], axis=0)
        pr_head[:, lanes], pr_tail[:, lanes] = halves(t_re)
        pi_head[:, lanes], pi_tail[:, lanes] = halves(t_im)
        return 0

    lax.fori_loop(0, WIDE // 128, one_chunk, 0)

    for j in range(WIDE // FILT):
        lanes = slice(FILT * j, FILT * j + FILT)
        both_head, both_tail = halves(jnp.concatenate([row_re[:, lanes], row_im[:, lanes]], axis=0))
        full = dot3(both_head, both_tail, *lead_tables(lanes, pr_head, pr_tail, pi_head, pi_tail), 1)
        full_re = full[0:8, 0:128] - full[8:16, 128:256]
        full_im = full[0:8, 128:256] + full[8:16, 0:128]
        response[j : j + 1, :] = full_re[ROW_GAIN : ROW_GAIN + 1]
        response[8 + j : 9 + j, :] = full_im[ROW_GAIN : ROW_GAIN + 1]


def delayed(row):
    lag = lax.broadcasted_iota(jnp.int32, (128, 128), 1) - lax.broadcasted_iota(
        jnp.int32, (128, 128), 0
    )
    rolled = pltpu.roll(jnp.broadcast_to(row, (128, 128)), 0, 1, stride=1, stride_axis=0)
    return jnp.where(lag >= 0, rolled, 0.0)


def column_kernel(
    place, x, flip, pr_head, pr_tail, pi_head, pi_tail, row_re, row_im, wr, wi, vr, vi,
    sent, turned, lhs,
):
    zi, xc = place[0], place[1]
    turned[...] = dot(jnp.concatenate(halves(x[...]), axis=0), flip[...])
    for q in range(8):
        rows = [turned[pl.ds(256 * h + 7 - q, 32, stride=8), :].astype(BF16) for h in (0, 1, 0)]
        lhs[32 * q : 32 * q + 32, :] = jnp.concatenate(rows, axis=1)
    own = lax.broadcasted_iota(jnp.int32, (8, 256), 0) == zi

    def one_part(part, _):
        lanes = pl.ds(pl.multiple_of(part * 256, 256), 256)
        e_re, e_im = (
            dot(lhs[...], jnp.concatenate([head[:, lanes], head[:, lanes], tail[:, lanes]], axis=0))
            for head, tail in ((pr_head, pr_tail), (pi_head, pi_tail))
        )
        step_re = row_re[ROW_128 : ROW_128 + 1, lanes]
        step_im = row_im[ROW_128 : ROW_128 + 1, lanes]
        s_re, s_im = e_re[224:256], e_im[224:256]
        for q in range(6, -1, -1):
            s_re, s_im = cmul(s_re, s_im, step_re, step_im)
            s_re = s_re + e_re[32 * q : 32 * q + 32]
            s_im = s_im + e_im[32 * q : 32 * q + 32]
        w_re, w_im = wr[:, lanes], wi[:, lanes]
        before_re, before_im, own_re, own_im = [], [], [], []
        for d in range(4):
            d_re, d_im = s_re[8 * d : 8 * d + 8], s_im[8 * d : 8 * d + 8]
            t_re, t_im = cmul(d_re, d_im, w_re, w_im)
            before_re.append(jnp.sum(t_re, axis=0, keepdims=True))
            before_im.append(jnp.sum(t_im, axis=0, keepdims=True))
            own_re.append(jnp.sum(jnp.where(own, d_re, 0.0), axis=0, keepdims=True))
            own_im.append(jnp.sum(jnp.where(own, d_im, 0.0), axis=0, keepdims=True))
        b_re, b_im, o_re, o_im = (
            jnp.concatenate(v, axis=0) for v in (before_re, before_im, own_re, own_im)
        )
        i_re, i_im = cmul(
            b_re, b_im,
            row_re[ROW_8192 : ROW_8192 + 1, lanes], row_im[ROW_8192 : ROW_8192 + 1, lanes],
        )
        i_re, i_im = i_re + o_re, i_im + o_im
        for p in range(8):
            t_re, t_im = cmul(
                jnp.where(xc < p, i_re, b_re), jnp.where(xc < p, i_im, b_im),
                vr[p : p + 1, lanes], vi[p : p + 1, lanes],
            )
            sent[p, :, lanes] = jnp.concatenate([t_re, t_im], axis=0)
        return 0

    lax.fori_loop(0, WIDE // 256, one_part, 0, unroll=UNROLL)

    shard = jnp.where(xc == 0, zi + 1, zi)
    inside = shard < 8
    row = jnp.minimum(shard, 7) * 8
    halo = jnp.concatenate(
        [x[pl.ds(row + 64 * d, 1), :] for d in range(4)] + [jnp.zeros((4, 128), F32)],
        axis=0,
    )
    halo = jnp.where(inside, halo, 0.0)
    for p in range(8):
        sent[p, :, WIDE : WIDE + 128] = halo


def local_kernel(
    place, x, flip, pr_head, pr_tail, pi_head, pi_tail, response,
    e_re, e_im, direct, blocks,
):
    zi = place[0]
    for m in range(8):
        for d in range(4):
            row = 4 * m + d
            blocks[row : row + 1, :] = x[pl.ds(64 * d + 8 * zi + m, 1), :]
    n_head, n_tail = halves(blocks[...])
    x_head, x_tail = (dot(v, flip[...]).astype(BF16) for v in (n_head, n_tail))
    for j in range(WIDE // FILT):
        lanes = slice(FILT * j, FILT * j + FILT)
        e_re[:, lanes] = dot3(x_head, x_tail, pr_head[:, lanes], pr_tail[:, lanes])
        e_im[:, lanes] = dot3(x_head, x_tail, pi_head[:, lanes], pi_tail[:, lanes])
        matrices = [delayed(response[row : row + 1, :]) for row in (j, 8 + j)]
        direct[j] = dot3(n_head, n_tail, *halves(jnp.concatenate(matrices, axis=1)))


def peak_kernel(
    place, delay, antenna, got, e_re, e_im, direct, response,
    pr_head, pr_tail, pi_head, pi_tail, row_re, row_im,
    out, s_re, s_im, snr, grouped, shifted,
):
    zi, xc = place[0], place[1]
    last = jnp.logical_and(zi == 7, xc == 7)
    halo = got[(xc + 1) & 7, :, WIDE : WIDE + 128]
    h_head, h_tail = halves(response[...])

    def one_part(part, _):
        lanes = pl.ds(pl.multiple_of(part * FILT, FILT), FILT)
        l_re, l_im = e_re[:, lanes], e_im[:, lanes]
        q = got[0, :, lanes]
        for p in range(1, 8):
            q = q + got[p, :, lanes]
        q_re, q_im = q[0:4], q[4:8]
        step_re = row_re[ROW_128 : ROW_128 + 1, lanes]
        step_im = row_im[ROW_128 : ROW_128 + 1, lanes]
        g_re = row_re[ROW_LEAD : ROW_LEAD + 1, lanes]
        g_im = row_im[ROW_LEAD : ROW_LEAD + 1, lanes]
        for m in range(9):
            t_re, t_im = cmul(q_re, q_im, g_re, g_im)
            if m == 8:
                t_re = jnp.where(last, 0.0, t_re)
                t_im = jnp.where(last, 0.0, t_im)
            s_re[4 * m : 4 * m + 4, lanes] = t_re
            s_im[4 * m : 4 * m + 4, lanes] = t_im
            if m < 8:
                q_re, q_im = cmul(q_re, q_im, step_re, step_im)
                q_re = q_re + l_re[4 * m : 4 * m + 4]
                q_im = q_im + l_im[4 * m : 4 * m + 4]
        both_head, both_tail = halves(jnp.concatenate([s_re[:, lanes], s_im[:, lanes]], axis=0))
        full = dot3(both_head, both_tail, *lead_tables(lanes, pr_head, pr_tail, pi_head, pi_tail), 1)
        own = direct[part]
        f_re = full[0:40, 0:128] - full[40:80, 128:256]
        f_im = full[0:40, 128:256] + full[40:80, 0:128]
        snr[0, 0:32, :], snr[0, 32:40, :] = f_re[0:32] + own[:, 0:128], f_re[32:40]
        snr[1, 0:32, :], snr[1, 32:40, :] = f_im[0:32] + own[:, 128:256], f_im[32:40]
        for c in range(2):
            for d in range(4):
                grouped[c, d, pl.ds(part, 9, stride=8), :] = snr[c, pl.ds(d, 9, stride=4), :]
        return 0

    grouped[:, :, 72:128, :] = jnp.zeros((2, 4, 56, 128), F32)
    s_re[36:40, :] = jnp.zeros((4, WIDE), F32)
    s_im[36:40, :] = jnp.zeros((4, WIDE), F32)
    lax.fori_loop(0, WIDE // 256, one_part, 0, unroll=UNROLL)

    for d in range(4):
        ahead = dot3(h_head, h_tail, *halves(delayed(halo[d : d + 1])))
        for c in range(2):
            grouped[c, d, 64:72, :] = grouped[c, d, 64:72, :] + ahead[8 * c : 8 * c + 8]

    early = lax.broadcasted_iota(jnp.int32, (64, 128), 1) < 64
    for c in range(2):
        for d in range(4):
            t = grouped[c, d].T
            top, low = t[0:64], t[64:128]
            ahead_top, ahead_low = pltpu.roll(top, 120, 1), pltpu.roll(low, 120, 1)
            shifted[c, d, 0:64, :] = jnp.where(early, top, pltpu.roll(low, 64, 1))
            shifted[c, d, 64:128, :] = jnp.where(early, low, pltpu.roll(top, 56, 1))
            shifted[c, d, 128:192, :] = jnp.where(early, ahead_top, pltpu.roll(low, 56, 1))

    def one_sky(s, best):
        total = [None] * 4
        for d in range(4):
            rows = pl.ds(delay[4 * s + d], 64)
            for c in range(2):
                piece = shifted[c, d, rows, :]
                for p in range(2):
                    term = antenna[8 * s + 4 * p + d] * piece
                    k = 2 * p + c
                    total[k] = term if total[k] is None else total[k] + term
        energy = (total[0] * total[0] + total[1] * total[1]) + (
            total[2] * total[2] + total[3] * total[3]
        )
        return jnp.maximum(best, energy)

    best = lax.fori_loop(0, SKY, one_sky, jnp.zeros((64, 128), F32), unroll=2)
    turned = best.T
    for m in range(8):
        out[:, 128 * m : 128 * m + 128] = jnp.concatenate(
            [turned[8 * m : 8 * m + 8], turned[64 + 8 * m : 72 + 8 * m]], axis=1
        )


def call(kernel, n_scalar, n_vector, shapes, scratch):
    scalar, vector = (pl.BlockSpec(memory_space=m) for m in (pltpu.SMEM, pltpu.VMEM))
    return pl.pallas_call(
        kernel,
        out_shape=[jax.ShapeDtypeStruct(*s) for s in shapes],
        in_specs=[scalar] * n_scalar + [vector] * n_vector,
        out_specs=[vector] * len(shapes),
        scratch_shapes=[pltpu.VMEM(*s) for s in scratch],
        compiler_params=pltpu.CompilerParams(vmem_limit_bytes=VMEM_LIMIT),
    )


TABLE, EIGHT = ((128, WIDE), BF16), ((8, WIDE), F32)
PREPARED = [TABLE] * 4 + [EIGHT] * 6 + [((16, 128), F32)]
LOCAL = [((32, WIDE), F32), ((32, WIDE), F32), ((8, 32, 256), F32)]


def prepare(*args):
    return call(prepare_kernel, 1, 4, PREPARED, [((4, 16, 128), F32)])(*args)


def of_column(*args):
    scratch = [((512, 128), F32), ((256, 384), BF16)]
    return call(column_kernel, 1, 12, [((8, 8, WIDE + 128), F32)], scratch)(*args)[0]


def of_device(*args):
    return call(local_kernel, 1, 7, LOCAL, [((32, 128), F32)])(*args)


def to_peak(*args):
    scratch = [
        ((40, WIDE), F32), ((40, WIDE), F32), ((2, 40, 128), F32), ((2, 4, 128, 128), F32),
        ((2, 4, 192, 128), F32),
    ]
    return call(peak_kernel, 3, 11, [((8, 1024), F32)], scratch)(*args)[0]


def shards(strain, decay_rate, frequency, gain, member, sky_delay, antenna):
    sent = jnp.broadcast_to(strain.reshape(1, 8, 128), (32, 8, 128))
    column = lax.all_to_all(sent, ("det", "z"), 0, 0, tiled=True).reshape(256, 128)
    plane = 2 * lax.axis_index("x") + lax.axis_index("core")
    place = jnp.stack([lax.axis_index("z"), plane, lax.axis_index("det")]).astype(jnp.int32)
    flip = jnp.asarray(np.eye(128, dtype=np.float32)[::-1], dtype=BF16)
    prh, prt, pih, pit, rr, ri, wr, wi, vr, vi, response = prepare(
        place, decay_rate.reshape(64, 128), frequency.reshape(64, 128), gain, member.reshape(64, 128)
    )
    partial = of_column(place, column, flip, prh, prt, pih, pit, rr, ri, wr, wi, vr, vi)
    got = lax.all_to_all(partial, ("x", "core"), 0, 0, tiled=True)
    e_re, e_im, direct = of_device(place, column, flip, prh, prt, pih, pit, response)
    return to_peak(
        place, sky_delay.reshape(-1), antenna.reshape(-1),
        got, e_re, e_im, direct, response, prh, prt, pih, pit, rr, ri,
    )


def solution(mesh):
    fine = Mesh(mesh.devices.reshape(8, 4, 2, 4), ("z", "x", "core", "det"))
    time = ("z", "x", "core")
    in_specs = (P("det", time), P(), P(), P(), P(), P(), P())
    return jax.shard_map(
        shards, mesh=fine, in_specs=in_specs, out_specs=P("det", time), check_vma=False
    )
```

```python
import math

import jax
import jax.numpy as jnp
import numpy as np
from jax import lax
from jax.experimental import pallas as pl
from jax.experimental.pallas import tpu as pltpu
from jax.sharding import Mesh, PartitionSpec as P

FILT = 256
SKY = 64
WIDE = 8 * FILT
F32, BF16 = jnp.float32, jnp.bfloat16

TURN = 1.0 / (2.0 * math.pi)
TURN_HEAD = math.floor(TURN * 2**14) / 2**14
TURN_TAIL = TURN - TURN_HEAD

ROW_128, ROW_8192, ROW_GAIN, ROW_LEAD = 0, 1, 2, 3

VMEM_LIMIT = 16 * 2**20
UNROLL = True


def taylor(first, start, count):
    return [
        first * (-1) ** k * math.pi ** (2 * k + start) / math.factorial(2 * k + start)
        for k in range(count)
    ]


SINE, COSINE = taylor(1.0, 1, 8), taylor(1.0, 0, 9)


def horner(coefficients, square):
    total = jnp.full(square.shape, coefficients[-1], F32)
    for c in coefficients[-2::-1]:
        total = total * square + c
    return total


def cmul(ar, ai, br, bi):
    return ar * br - ai * bi, ar * bi + ai * br


def halves(x):
    head = x.astype(BF16)
    return head, (x - head.astype(F32)).astype(BF16)


def dot(a, b, contract_b=0):
    return lax.dot_general(
        a, b, (((1,), (contract_b,)), ((), ())), preferred_element_type=F32
    )


def dot3(a_head, a_tail, b_head, b_tail, contract_b=0):
    rows = a_head.shape[0]
    both = dot(jnp.concatenate([a_head, a_tail], axis=0), b_head, contract_b)
    return both[:rows] + both[rows:] + dot(a_head, b_tail, contract_b)


def lead_tables(lanes, pr_head, pr_tail, pi_head, pi_tail):
    return (
        jnp.concatenate([pr_head[:, lanes], pi_head[:, lanes]], axis=0),
        jnp.concatenate([pr_tail[:, lanes], pi_tail[:, lanes]], axis=0),
    )


def prepare_kernel(
    place, decay, frequency, gain, member,
    pr_head, pr_tail, pi_head, pi_tail, row_re, row_im, wr, wi, vr, vi, response,
    par,
):
    zi, xc, det = place[0], place[1], place[2]

    index = [
        member[pl.ds(pl.multiple_of(16 * det + 8 * half, 8), 8), :] for half in range(2)
    ]
    high, low = [v >> 7 for v in index], [v & 127 for v in index]

    def one_row(r, carried):
        lanes = pl.ds(pl.multiple_of(r * 128, 128), 128)
        values = (
            decay[pl.ds(r, 1), :],
            frequency[pl.ds(r, 1), :],
            gain[0:1, lanes],
            gain[1:2, lanes],
        )
        spread = [jnp.broadcast_to(v, (8, 128)) for v in values]
        return tuple(
            jnp.where(
                high[h] == r,
                jnp.take_along_axis(spread[k], low[h], axis=1),
                carried[4 * h + k],
            )
            for h in range(2)
            for k in range(4)
        )

    nothing = jnp.zeros((8, 128), F32)
    found = lax.fori_loop(0, 64, one_row, (nothing,) * 8, unroll=8)
    for h in range(2):
        for k in range(4):
            par[k, 8 * h : 8 * h + 8, :] = found[4 * h + k]

    power = jnp.left_shift(1, lax.broadcasted_iota(jnp.int32, (16, 128), 0)).astype(F32)
    place8 = lax.broadcasted_iota(jnp.int32, (8, 128), 0)
    ahead_z = zi - 1 - place8
    ahead_x = jnp.where(place8 < 4, 2 * place8 - 1, 2 * place8 + 2 * (xc & 1) - 10) & 7

    def choose(exponent, rows, re, im):
        out_re = jnp.ones((8, 128), F32)
        out_im = jnp.zeros((8, 128), F32)
        for bit, row in enumerate(rows):
            new_re, new_im = cmul(out_re, out_im, re[row : row + 1], im[row : row + 1])
            on = (exponent >> bit) & 1 == 1
            out_re = jnp.where(on, new_re, out_re)
            out_im = jnp.where(on, new_im, out_im)
        return out_re, out_im

    def one_chunk(c, _):
        lanes = pl.ds(pl.multiple_of(c * 128, 128), 128)
        f = par[1, pl.ds(c, 1), :]
        f_head = jnp.floor(f * 2048.0) * (1.0 / 2048.0)
        f_tail = f - f_head
        first = power * (f_head * TURN_HEAD)
        second = power * (f_head * TURN_TAIL + f_tail * TURN)
        turn = (first - jnp.floor(first + 0.5)) + (second - jnp.floor(second + 0.5))
        turn = turn - jnp.floor(turn + 0.5)
        square = turn * turn
        sine = turn * horner(SINE, square)
        cosine = horner(COSINE, square)
        size = jnp.exp(-power * par[0, pl.ds(c, 1), :])
        re = size * (1.0 - 2.0 * sine * sine)
        im = size * (2.0 * sine * cosine)
        g_re, g_im = par[2, pl.ds(c, 1), :], par[3, pl.ds(c, 1), :]
        l_re, l_im = cmul(g_re, g_im, re[0:1], im[0:1])
        empty = jnp.zeros((4, 128), F32)
        row_re[:, lanes] = jnp.concatenate([re[7:8], re[13:14], g_re, l_re, empty], axis=0)
        row_im[:, lanes] = jnp.concatenate([im[7:8], im[13:14], g_im, l_im, empty], axis=0)
        w_re, w_im = choose(ahead_z, (13, 14, 15), re, im)
        wr[:, lanes] = jnp.where(ahead_z >= 0, w_re, 0.0)
        wi[:, lanes] = jnp.where(ahead_z >= 0, w_im, 0.0)
        vr[:, lanes], vi[:, lanes] = choose(ahead_x, (10, 11, 12), re, im)
        t_re, t_im = choose(place8, (0, 1, 2), re, im)
        for row in range(3, 7):
            n_re, n_im = cmul(t_re, t_im, re[row : row + 1], im[row : row + 1])
            t_re = jnp.concatenate([t_re, n_re], axis=0)
            t_im = jnp.concatenate([t_im, n_im], axis=0)
        pr_head[:, lanes], pr_tail[:, lanes] = halves(t_re)
        pi_head[:, lanes], pi_tail[:, lanes] = halves(t_im)
        return 0

    lax.fori_loop(0, WIDE // 128, one_chunk, 0)

    for j in range(WIDE // FILT):
        lanes = slice(FILT * j, FILT * j + FILT)
        both_head, both_tail = halves(jnp.concatenate([row_re[:, lanes], row_im[:, lanes]], axis=0))
        full = dot3(both_head, both_tail, *lead_tables(lanes, pr_head, pr_tail, pi_head, pi_tail), 1)
        full_re = full[0:8, 0:128] - full[8:16, 128:256]
        full_im = full[0:8, 128:256] + full[8:16, 0:128]
        response[j : j + 1, :] = full_re[ROW_GAIN : ROW_GAIN + 1]
        response[8 + j : 9 + j, :] = full_im[ROW_GAIN : ROW_GAIN + 1]


def delayed(row):
    lag = lax.broadcasted_iota(jnp.int32, (128, 128), 1) - lax.broadcasted_iota(
        jnp.int32, (128, 128), 0
    )
    rolled = pltpu.roll(jnp.broadcast_to(row, (128, 128)), 0, 1, stride=1, stride_axis=0)
    return jnp.where(lag >= 0, rolled, 0.0)


def column_kernel(
    place, x, flip, pr_head, pr_tail, pi_head, pi_tail, row_re, row_im, wr, wi,
    states, turned, lhs,
):
    zi, xc = place[0], place[1]
    turned[...] = dot(jnp.concatenate(halves(x[...]), axis=0), flip[...])
    for q in range(8):
        rows = [turned[pl.ds(256 * h + 7 - q, 32, stride=8), :].astype(BF16) for h in (0, 1, 0)]
        lhs[32 * q : 32 * q + 32, :] = jnp.concatenate(rows, axis=1)
    own = lax.broadcasted_iota(jnp.int32, (8, 256), 0) == zi

    def one_part(part, _):
        lanes = pl.ds(pl.multiple_of(part * 256, 256), 256)
        e_re, e_im = (
            dot(lhs[...], jnp.concatenate([head[:, lanes], head[:, lanes], tail[:, lanes]], axis=0))
            for head, tail in ((pr_head, pr_tail), (pi_head, pi_tail))
        )
        step_re = row_re[ROW_128 : ROW_128 + 1, lanes]
        step_im = row_im[ROW_128 : ROW_128 + 1, lanes]
        s_re, s_im = e_re[224:256], e_im[224:256]
        for q in range(6, -1, -1):
            s_re, s_im = cmul(s_re, s_im, step_re, step_im)
            s_re = s_re + e_re[32 * q : 32 * q + 32]
            s_im = s_im + e_im[32 * q : 32 * q + 32]
        w_re, w_im = wr[:, lanes], wi[:, lanes]
        before_re, before_im, own_re, own_im = [], [], [], []
        for d in range(4):
            d_re, d_im = s_re[8 * d : 8 * d + 8], s_im[8 * d : 8 * d + 8]
            t_re, t_im = cmul(d_re, d_im, w_re, w_im)
            before_re.append(jnp.sum(t_re, axis=0, keepdims=True))
            before_im.append(jnp.sum(t_im, axis=0, keepdims=True))
            own_re.append(jnp.sum(jnp.where(own, d_re, 0.0), axis=0, keepdims=True))
            own_im.append(jnp.sum(jnp.where(own, d_im, 0.0), axis=0, keepdims=True))
        b_re, b_im, o_re, o_im = (
            jnp.concatenate(v, axis=0) for v in (before_re, before_im, own_re, own_im)
        )
        i_re, i_im = cmul(
            b_re, b_im,
            row_re[ROW_8192 : ROW_8192 + 1, lanes], row_im[ROW_8192 : ROW_8192 + 1, lanes],
        )
        states[0, :, lanes] = jnp.concatenate([b_re, b_im], axis=0)
        states[1, :, lanes] = jnp.concatenate([i_re + o_re, i_im + o_im], axis=0)
        return 0

    lax.fori_loop(0, WIDE // 256, one_part, 0, unroll=UNROLL)

    shard = jnp.where(xc == 0, zi + 1, zi)
    inside = shard < 8
    row = jnp.minimum(shard, 7) * 8
    halo = jnp.concatenate(
        [x[pl.ds(row + 64 * d, 1), :] for d in range(4)] + [jnp.zeros((4, 128), F32)],
        axis=0,
    )
    halo = jnp.where(inside, halo, 0.0)
    for p in range(2):
        states[p, :, WIDE : WIDE + 128] = halo


def chip_kernel(place, mine, other, vr, vi, *sent):
    x, core = place[1] >> 1, place[1] & 1
    for k in range(4):
        target = 2 * ((x + k) & 3) + core
        for part in range(WIDE // 256):
            lanes = slice(256 * part, 256 * part + 256)
            total = None
            for states, column, row in ((mine, 2 * x + core, k), (other, 2 * x + 1 - core, 4 + k)):
                state = states[jnp.where(column < target, 1, 0), :, lanes]
                term = cmul(
                    state[0:4], state[4:8], vr[row : row + 1, lanes], vi[row : row + 1, lanes]
                )
                total = term if total is None else (total[0] + term[0], total[1] + term[1])
            sent[k][:, lanes] = jnp.concatenate(total, axis=0)
        sent[k][:, WIDE : WIDE + 128] = other[0, :, WIDE : WIDE + 128]


def local_kernel(
    place, x, flip, pr_head, pr_tail, pi_head, pi_tail, row_re, row_im, response,
    local, blocks, s_all,
):
    zi = place[0]
    for m in range(8):
        for d in range(4):
            row = 4 * m + d
            blocks[row : row + 1, :] = x[pl.ds(64 * d + 8 * zi + m, 1), :]
    n_head, n_tail = halves(blocks[...])
    x_head, x_tail = (dot(v, flip[...]).astype(BF16) for v in (n_head, n_tail))
    s_all[...] = jnp.zeros((80, WIDE), F32)
    for j in range(WIDE // FILT):
        lanes = slice(FILT * j, FILT * j + FILT)
        l_re = dot3(x_head, x_tail, pr_head[:, lanes], pr_tail[:, lanes])
        l_im = dot3(x_head, x_tail, pi_head[:, lanes], pi_tail[:, lanes])
        g_re, g_im, step_re, step_im = (
            v[row : row + 1, lanes] for row in (ROW_LEAD, ROW_128) for v in (row_re, row_im)
        )
        q_re, q_im = l_re[0:4], l_im[0:4]
        for m in range(1, 9):
            s_all[4 * m : 4 * m + 4, lanes], s_all[40 + 4 * m : 44 + 4 * m, lanes] = cmul(
                q_re, q_im, g_re, g_im
            )
            if m < 8:
                q_re, q_im = cmul(q_re, q_im, step_re, step_im)
                q_re = q_re + l_re[4 * m : 4 * m + 4]
                q_im = q_im + l_im[4 * m : 4 * m + 4]
        full = dot3(
            *halves(s_all[:, lanes]), *lead_tables(lanes, pr_head, pr_tail, pi_head, pi_tail), 1
        )
        matrices = [delayed(response[row : row + 1, :]) for row in (j, 8 + j)]
        own = dot3(n_head, n_tail, *halves(jnp.concatenate(matrices, axis=1)))
        f_re = full[0:40, 0:128] - full[40:80, 128:256]
        f_im = full[0:40, 128:256] + full[40:80, 0:128]
        local[j, 0, 0:32, :], local[j, 0, 32:40, :] = f_re[0:32] + own[:, 0:128], f_re[32:40]
        local[j, 1, 0:32, :], local[j, 1, 32:40, :] = f_im[0:32] + own[:, 128:256], f_im[32:40]


def peak_kernel(
    place, delay, antenna, got0, got1, got2, got3, local, response,
    pr_head, pr_tail, pi_head, pi_tail, row_re, row_im,
    out, s_all, snr, grouped, shifted,
):
    zi, xc = place[0], place[1]
    keep = jnp.where(jnp.logical_and(zi == 7, xc == 7), 0.0, 1.0)
    ahead_lanes = slice(WIDE, WIDE + 128)
    halo = jnp.where((xc & 1) == 0, got0[:, ahead_lanes], got3[:, ahead_lanes])
    h_head, h_tail = halves(response[...])
    s_all[...] = jnp.zeros((80, WIDE), F32)
    grouped[:, :, 72:128, :] = jnp.zeros((2, 4, 56, 128), F32)

    for j in range(WIDE // FILT):
        lanes = slice(FILT * j, FILT * j + FILT)
        q = (got0[:, lanes] + got1[:, lanes]) + (got2[:, lanes] + got3[:, lanes])
        g_re, g_im, step_re, step_im = (
            v[row : row + 1, lanes] for row in (ROW_LEAD, ROW_128) for v in (row_re, row_im)
        )
        q_re, q_im = cmul(q[0:4], q[4:8], g_re, g_im)
        for m in range(9):
            s_all[4 * m : 4 * m + 4, lanes] = q_re
            s_all[40 + 4 * m : 44 + 4 * m, lanes] = q_im
            q_re, q_im = cmul(q_re, q_im, step_re, step_im)
        full = dot3(
            *halves(s_all[:, lanes]), *lead_tables(lanes, pr_head, pr_tail, pi_head, pi_tail), 1
        )
        f_re = full[0:40, 0:128] - full[40:80, 128:256] + local[j, 0]
        f_im = full[0:40, 128:256] + full[40:80, 0:128] + local[j, 1]
        for c, f in enumerate((f_re, f_im)):
            snr[c, 0:32, :], snr[c, 32:40, :] = f[0:32], f[32:40] * keep
            for d in range(4):
                grouped[c, d, pl.ds(j, 9, stride=8), :] = snr[c, pl.ds(d, 9, stride=4), :]

    for d in range(4):
        ahead = dot3(h_head, h_tail, *halves(delayed(halo[d : d + 1])))
        for c in range(2):
            grouped[c, d, 64:72, :] = grouped[c, d, 64:72, :] + ahead[8 * c : 8 * c + 8]

    early = lax.broadcasted_iota(jnp.int32, (64, 128), 1) < 64
    for c in range(2):
        for d in range(4):
            t = grouped[c, d].T
            top, low = t[0:64], t[64:128]
            ahead_top, ahead_low = pltpu.roll(top, 120, 1), pltpu.roll(low, 120, 1)
            shifted[c, d, 0:64, :] = jnp.where(early, top, pltpu.roll(low, 64, 1))
            shifted[c, d, 64:128, :] = jnp.where(early, low, pltpu.roll(top, 56, 1))
            shifted[c, d, 128:192, :] = jnp.where(early, ahead_top, pltpu.roll(low, 56, 1))

    def one_sky(s, best):
        total = [None] * 4
        for d in range(4):
            rows = pl.ds(delay[4 * s + d], 64)
            for c in range(2):
                piece = shifted[c, d, rows, :]
                for p in range(2):
                    term = antenna[8 * s + 4 * p + d] * piece
                    k = 2 * p + c
                    total[k] = term if total[k] is None else total[k] + term
        energy = (total[0] * total[0] + total[1] * total[1]) + (
            total[2] * total[2] + total[3] * total[3]
        )
        return jnp.maximum(best, energy)

    best = lax.fori_loop(0, SKY, one_sky, jnp.zeros((64, 128), F32), unroll=2)
    turned = best.T
    for m in range(8):
        out[:, 128 * m : 128 * m + 128] = jnp.concatenate(
            [turned[8 * m : 8 * m + 8], turned[64 + 8 * m : 72 + 8 * m]], axis=1
        )


def call(kernel, n_scalar, n_vector, shapes, scratch):
    scalar, vector = (pl.BlockSpec(memory_space=m) for m in (pltpu.SMEM, pltpu.VMEM))
    return pl.pallas_call(
        kernel,
        out_shape=[jax.ShapeDtypeStruct(*s) for s in shapes],
        in_specs=[scalar] * n_scalar + [vector] * n_vector,
        out_specs=[vector] * len(shapes),
        scratch_shapes=[pltpu.VMEM(*s) for s in scratch],
        compiler_params=pltpu.CompilerParams(vmem_limit_bytes=VMEM_LIMIT),
    )


TABLE, EIGHT = ((128, WIDE), BF16), ((8, WIDE), F32)
PREPARED = [TABLE] * 4 + [EIGHT] * 6 + [((16, 128), F32)]
STATE = ((8, WIDE + 128), F32)


def prepare(*args):
    return call(prepare_kernel, 1, 4, PREPARED, [((4, 16, 128), F32)])(*args)


def of_column(*args):
    scratch = [((512, 128), F32), ((256, 384), BF16)]
    return call(column_kernel, 1, 10, [((2, 8, WIDE + 128), F32)], scratch)(*args)[0]


def of_chip(*args):
    return call(chip_kernel, 1, 4, [STATE] * 4, [])(*args)


def of_device(*args):
    scratch = [((32, 128), F32), ((80, WIDE), F32)]
    return call(local_kernel, 1, 9, [((8, 2, 40, 128), F32)], scratch)(*args)[0]


def to_peak(*args):
    scratch = [
        ((80, WIDE), F32), ((2, 40, 128), F32), ((2, 4, 128, 128), F32), ((2, 4, 192, 128), F32),
    ]
    return call(peak_kernel, 3, 12, [((8, 1024), F32)], scratch)(*args)[0]


def shards(strain, decay_rate, frequency, gain, member, sky_delay, antenna):
    sent = jnp.broadcast_to(strain.reshape(1, 8, 128), (32, 8, 128))
    column = lax.all_to_all(sent, ("det", "z"), 0, 0, tiled=True).reshape(256, 128)
    plane = 2 * lax.axis_index("x") + lax.axis_index("core")
    place = jnp.stack([lax.axis_index("z"), plane, lax.axis_index("det")]).astype(jnp.int32)
    flip = jnp.asarray(np.eye(128, dtype=np.float32)[::-1], dtype=BF16)
    *tables, rr, ri, wr, wi, vr, vi, response = prepare(
        place, decay_rate.reshape(64, 128), frequency.reshape(64, 128), gain, member.reshape(64, 128)
    )
    mine = of_column(place, column, flip, *tables, rr, ri, wr, wi)
    other = lax.ppermute(mine, "core", [(0, 1), (1, 0)])
    first, *rest = of_chip(place, mine, other, vr, vi)
    got = [
        lax.ppermute(v, "x", [(x, (x + k) % 4) for x in range(4)]) for k, v in enumerate(rest, 1)
    ]
    local = of_device(place, column, flip, *tables, rr, ri, response)
    return to_peak(
        place, sky_delay.reshape(-1), antenna.reshape(-1),
        first, *got, local, response, *tables, rr, ri,
    )


def solution(mesh):
    fine = Mesh(mesh.devices.reshape(8, 4, 2, 4), ("z", "x", "core", "det"))
    time = ("z", "x", "core")
    in_specs = (P("det", time), P(), P(), P(), P(), P(), P())
    return jax.shard_map(
        shards, mesh=fine, in_specs=in_specs, out_specs=P("det", time), check_vma=False
    )
```

```python
import functools
import math

import jax
import jax.numpy as jnp
import numpy as np
from jax import lax
from jax.experimental import pallas as pl
from jax.experimental.pallas import tpu as pltpu
from jax.sharding import Mesh, PartitionSpec as P

FILT = 256
SKY = 64
WIDE = 8 * FILT
F32, BF16 = jnp.float32, jnp.bfloat16

TURN = 1.0 / (2.0 * math.pi)
TURN_HEAD = math.floor(TURN * 2**14) / 2**14
TURN_TAIL = TURN - TURN_HEAD

ROW_128, ROW_1024, ROW_8192, ROW_GAIN, ROW_LEAD = 0, 1, 2, 3, 4

VMEM_LIMIT = 16 * 2**20
UNROLL = True
EARLY = 3


def taylor(first, start, count):
    return [
        first * (-1) ** k * math.pi ** (2 * k + start) / math.factorial(2 * k + start)
        for k in range(count)
    ]


SINE, COSINE = taylor(1.0, 1, 8), taylor(1.0, 0, 9)


def horner(coefficients, square):
    total = jnp.full(square.shape, coefficients[-1], F32)
    for c in coefficients[-2::-1]:
        total = total * square + c
    return total


def cmul(ar, ai, br, bi):
    return ar * br - ai * bi, ar * bi + ai * br


def halves(x):
    head = x.astype(BF16)
    return head, (x - head.astype(F32)).astype(BF16)


def dot(a, b, contract_b=0):
    return lax.dot_general(
        a, b, (((1,), (contract_b,)), ((), ())), preferred_element_type=F32
    )


def dot3(a_head, a_tail, b_head, b_tail, contract_b=0):
    rows = a_head.shape[0]
    both = dot(jnp.concatenate([a_head, a_tail], axis=0), b_head, contract_b)
    return both[:rows] + both[rows:] + dot(a_head, b_tail, contract_b)


def lead_tables(lanes, pr_head, pr_tail, pi_head, pi_tail):
    return (
        jnp.concatenate([pr_head[:, lanes], pi_head[:, lanes]], axis=0),
        jnp.concatenate([pr_tail[:, lanes], pi_tail[:, lanes]], axis=0),
    )


def prepare_kernel(
    place, decay, frequency, gain, member, antenna, sky_delay,
    pr_head, pr_tail, pi_head, pi_tail, row_re, row_im, block_re, block_im, wr, wi, vr, vi, response,
    weight, delay, par,
):
    zi, xc, det = place[0], place[1], place[2]

    delay[...] = sky_delay[...]
    one, two = antenna[0:4, :], antenna[4:8, :]
    scale = jnp.maximum(jnp.abs(one[0:1]), jnp.abs(two[0:1]))
    divisor = jnp.where(scale > 0.0, scale, 1.0)
    a, b = jnp.where(scale > 0.0, one[0:1] / divisor, 1.0), two[0:1] / divisor
    size = jnp.sqrt(a * a + b * b)
    cosine, sine = a / size, b / size
    weight[...] = jnp.concatenate([cosine * one + sine * two, cosine * two - sine * one], axis=0)

    index = [
        member[pl.ds(pl.multiple_of(16 * det + 8 * half, 8), 8), :] for half in range(2)
    ]
    high, low = [v >> 7 for v in index], [v & 127 for v in index]

    def one_row(r, carried):
        lanes = pl.ds(pl.multiple_of(r * 128, 128), 128)
        values = (
            decay[pl.ds(r, 1), :],
            frequency[pl.ds(r, 1), :],
            gain[0:1, lanes],
            gain[1:2, lanes],
        )
        spread = [jnp.broadcast_to(v, (8, 128)) for v in values]
        return tuple(
            jnp.where(
                high[h] == r,
                jnp.take_along_axis(spread[k], low[h], axis=1),
                carried[4 * h + k],
            )
            for h in range(2)
            for k in range(4)
        )

    nothing = jnp.zeros((8, 128), F32)
    found = lax.fori_loop(0, 64, one_row, (nothing,) * 8, unroll=8)
    for h in range(2):
        for k in range(4):
            par[k, 8 * h : 8 * h + 8, :] = found[4 * h + k]

    power = jnp.left_shift(1, lax.broadcasted_iota(jnp.int32, (16, 128), 0)).astype(F32)
    place8 = lax.broadcasted_iota(jnp.int32, (8, 128), 0)
    ahead_z = zi - 1 - (lax.broadcasted_iota(jnp.int32, (32, 128), 0) >> 2)
    ahead_x = jnp.where(place8 < 4, 2 * place8 - 1, 2 * place8 + 2 * (xc & 1) - 10) & 7

    def choose(exponent, rows, re, im):
        out_re = jnp.ones(exponent.shape, F32)
        out_im = jnp.zeros(exponent.shape, F32)
        for bit, row in enumerate(rows):
            new_re, new_im = cmul(out_re, out_im, re[row : row + 1], im[row : row + 1])
            on = (exponent >> bit) & 1 == 1
            out_re = jnp.where(on, new_re, out_re)
            out_im = jnp.where(on, new_im, out_im)
        return out_re, out_im

    def one_chunk(c, _):
        lanes = pl.ds(pl.multiple_of(c * 128, 128), 128)
        f = par[1, pl.ds(c, 1), :]
        f_head = jnp.floor(f * 2048.0) * (1.0 / 2048.0)
        f_tail = f - f_head
        first = power * (f_head * TURN_HEAD)
        second = power * (f_head * TURN_TAIL + f_tail * TURN)
        turn = (first - jnp.floor(first + 0.5)) + (second - jnp.floor(second + 0.5))
        turn = turn - jnp.floor(turn + 0.5)
        square = turn * turn
        sine = turn * horner(SINE, square)
        cosine = horner(COSINE, square)
        size = jnp.exp(-power * par[0, pl.ds(c, 1), :])
        re = size * (1.0 - 2.0 * sine * sine)
        im = size * (2.0 * sine * cosine)
        g_re, g_im = par[2, pl.ds(c, 1), :], par[3, pl.ds(c, 1), :]
        l_re, l_im = cmul(g_re, g_im, re[0:1], im[0:1])
        empty = jnp.zeros((3, 128), F32)
        for single, v, g, lead in ((row_re, re, g_re, l_re), (row_im, im, g_im, l_im)):
            single[:, lanes] = jnp.concatenate(
                [v[7:8], v[10:11], v[13:14], g, lead, empty], axis=0
            )
        block_re[:, lanes], block_im[:, lanes] = choose(place8, (7, 8, 9), re, im)
        w_re, w_im = choose(ahead_z, (13, 14, 15), re, im)
        wr[:, lanes] = jnp.where(ahead_z >= 0, w_re, 0.0)
        wi[:, lanes] = jnp.where(ahead_z >= 0, w_im, 0.0)
        vr[:, lanes], vi[:, lanes] = choose(ahead_x, (10, 11, 12), re, im)
        t_re, t_im = choose(place8, (0, 1, 2), re, im)
        for row in range(3, 7):
            n_re, n_im = cmul(t_re, t_im, re[row : row + 1], im[row : row + 1])
            t_re = jnp.concatenate([t_re, n_re], axis=0)
            t_im = jnp.concatenate([t_im, n_im], axis=0)
        pr_head[:, lanes], pr_tail[:, lanes] = halves(t_re)
        pi_head[:, lanes], pi_tail[:, lanes] = halves(t_im)
        return 0

    lax.fori_loop(0, WIDE // 128, one_chunk, 0)

    for j in range(WIDE // FILT):
        lanes = slice(FILT * j, FILT * j + FILT)
        both_head, both_tail = halves(jnp.concatenate([row_re[:, lanes], row_im[:, lanes]], axis=0))
        full = dot3(both_head, both_tail, *lead_tables(lanes, pr_head, pr_tail, pi_head, pi_tail), 1)
        full_re = full[0:8, 0:128] - full[8:16, 128:256]
        full_im = full[0:8, 128:256] + full[8:16, 0:128]
        response[j : j + 1, :] = full_re[ROW_GAIN : ROW_GAIN + 1]
        response[8 + j : 9 + j, :] = full_im[ROW_GAIN : ROW_GAIN + 1]


def delayed(row):
    lag = lax.broadcasted_iota(jnp.int32, (128, 128), 1) - lax.broadcasted_iota(
        jnp.int32, (128, 128), 0
    )
    rolled = pltpu.roll(jnp.broadcast_to(row, (128, 128)), 0, 1, stride=1, stride_axis=0)
    return jnp.where(lag >= 0, rolled, 0.0)


def column_kernel(
    place, x, flip, pr_head, pr_tail, pi_head, pi_tail, row_re, row_im, wr, wi,
    states, turned, lhs,
):
    zi, xc = place[0], place[1]
    turned[...] = dot(jnp.concatenate(halves(x[...]), axis=0), flip[...])
    for q in range(8):
        rows = [turned[pl.ds(256 * h + 7 - q, 32, stride=8), :].astype(BF16) for h in (0, 1, 0)]
        lhs[32 * q : 32 * q + 32, :] = jnp.concatenate(rows, axis=1)
    own = (lax.broadcasted_iota(jnp.int32, (32, 256), 0) >> 2) == zi
    upper = lax.broadcasted_iota(jnp.int32, (8, 256), 0) < 4

    def over_shards(v):
        total = (v[0:8] + v[8:16]) + (v[16:24] + v[24:32])
        return total + pltpu.roll(total, 4, 0)

    def one_part(part, _):
        lanes = pl.ds(pl.multiple_of(part * 256, 256), 256)
        e_re, e_im = (
            dot(lhs[...], jnp.concatenate([head[:, lanes], head[:, lanes], tail[:, lanes]], axis=0))
            for head, tail in ((pr_head, pr_tail), (pi_head, pi_tail))
        )
        step_re = row_re[ROW_128 : ROW_128 + 1, lanes]
        step_im = row_im[ROW_128 : ROW_128 + 1, lanes]
        s_re, s_im = e_re[224:256], e_im[224:256]
        for q in range(6, -1, -1):
            s_re, s_im = cmul(s_re, s_im, step_re, step_im)
            s_re = s_re + e_re[32 * q : 32 * q + 32]
            s_im = s_im + e_im[32 * q : 32 * q + 32]
        b_re, b_im = (over_shards(v) for v in cmul(s_re, s_im, wr[:, lanes], wi[:, lanes]))
        o_re, o_im = (over_shards(jnp.where(own, v, 0.0)) for v in (s_re, s_im))
        i_re, i_im = cmul(
            b_re, b_im,
            row_re[ROW_8192 : ROW_8192 + 1, lanes], row_im[ROW_8192 : ROW_8192 + 1, lanes],
        )
        states[0, :, lanes] = jnp.where(upper, b_re, b_im)
        states[1, :, lanes] = jnp.where(upper, i_re + o_re, i_im + o_im)
        return 0

    lax.fori_loop(0, WIDE // 256, one_part, 0, unroll=UNROLL)

    shard = jnp.where(xc == 0, zi + 1, zi)
    inside = shard < 8
    row = jnp.minimum(shard, 7) * 32
    halo = jnp.concatenate(
        [x[pl.ds(row + 8 * d, 1), :] for d in range(4)] + [jnp.zeros((4, 128), F32)],
        axis=0,
    )
    halo = jnp.where(inside, halo, 0.0)
    for p in range(2):
        states[p, :, WIDE : WIDE + 128] = halo


def chip_kernel(place, mine, other, vr, vi, beside, *sent):
    del beside
    upper = lax.broadcasted_iota(jnp.int32, (8, 256), 0) < 4
    x, core = place[1] >> 1, place[1] & 1
    for k in range(4):
        target = 2 * ((x + k) & 3) + core
        for part in range(WIDE // 256):
            lanes = slice(256 * part, 256 * part + 256)
            total = None
            for states, column, row in ((mine, 2 * x + core, k), (other, 2 * x + 1 - core, 4 + k)):
                state = states[jnp.where(column < target, 1, 0), :, lanes]
                turn = vi[row : row + 1, lanes]
                term = state * vr[row : row + 1, lanes] + pltpu.roll(state, 4, 0) * jnp.where(
                    upper, -turn, turn
                )
                total = term if total is None else total + term
            sent[k][:, lanes] = total
        sent[k][:, WIDE : WIDE + 128] = other[0, :, WIDE : WIDE + 128]


def local_kernel(
    place, x, flip, pr_head, pr_tail, pi_head, pi_tail, row_re, row_im, block_re, block_im, response,
    local, *, first,
):
    zi = place[0]
    n_head, n_tail = halves(x[pl.ds(pl.multiple_of(32 * zi, 32), 32), :])
    x_head, x_tail = (dot(v, flip[...]).astype(BF16) for v in (n_head, n_tail))
    row8 = lax.broadcasted_iota(jnp.int32, (8, FILT), 0)
    for k in range(local.shape[0]):
        j = first + k
        lanes = slice(FILT * j, FILT * j + FILT)
        l_re = dot3(x_head, x_tail, pr_head[:, lanes], pr_tail[:, lanes])
        l_im = dot3(x_head, x_tail, pi_head[:, lanes], pi_tail[:, lanes])
        g_re, g_im = (v[ROW_LEAD : ROW_LEAD + 1, lanes] for v in (row_re, row_im))
        s_re, s_im, end_re, end_im = [], [], [], []
        for d in range(4):
            q_re, q_im = cmul(l_re[8 * d : 8 * d + 8], l_im[8 * d : 8 * d + 8], g_re, g_im)
            for step in (1, 2, 4):
                t_re, t_im = cmul(
                    pltpu.roll(q_re, step, 0), pltpu.roll(q_im, step, 0),
                    block_re[step : step + 1, lanes], block_im[step : step + 1, lanes],
                )
                q_re = q_re + jnp.where(row8 >= step, t_re, 0.0)
                q_im = q_im + jnp.where(row8 >= step, t_im, 0.0)
            s_re.append(jnp.where(row8 >= 1, pltpu.roll(q_re, 1, 0), 0.0))
            s_im.append(jnp.where(row8 >= 1, pltpu.roll(q_im, 1, 0), 0.0))
            end_re.append(q_re[7:8])
            end_im.append(q_im[7:8])
        none = [jnp.zeros((4, FILT), F32)]
        full = dot3(
            *halves(jnp.concatenate(s_re + end_re + none + s_im + end_im + none, axis=0)),
            *lead_tables(lanes, pr_head, pr_tail, pi_head, pi_tail), 1,
        )
        matrices = [delayed(response[row : row + 1, :]) for row in (j, 8 + j)]
        own = dot3(n_head, n_tail, *halves(jnp.concatenate(matrices, axis=1)))
        f_re = full[0:40, 0:128] - full[40:80, 128:256]
        f_im = full[0:40, 128:256] + full[40:80, 0:128]
        local[k, 0, 0:32, :], local[k, 0, 32:40, :] = f_re[0:32] + own[:, 0:128], f_re[32:40]
        local[k, 1, 0:32, :], local[k, 1, 32:40, :] = f_im[0:32] + own[:, 128:256], f_im[32:40]


def peak_kernel(
    place, delay, antenna, got0, got1, got2, got3, local0, local1, response,
    pr_head, pr_tail, pi_head, pi_tail, row_re, row_im, block_re, block_im,
    out, grouped, shifted,
):
    zi, xc = place[0], place[1]
    keep = jnp.where(jnp.logical_and(zi == 7, xc == 7), 0.0, 1.0)
    ahead_lanes = slice(WIDE, WIDE + 128)
    halo = jnp.where((xc & 1) == 0, got0[:, ahead_lanes], got3[:, ahead_lanes])
    h_head, h_tail = halves(response[...])
    bottom = lax.broadcasted_iota(jnp.int32, (8, 128), 0) == 7

    for j in range(WIDE // FILT):
        lanes = slice(FILT * j, FILT * j + FILT)
        q = (got0[:, lanes] + got1[:, lanes]) + (got2[:, lanes] + got3[:, lanes])
        single = [
            v[row : row + 1, lanes] for row in (ROW_LEAD, ROW_1024) for v in (row_re, row_im)
        ]
        q_re, q_im = cmul(q, pltpu.roll(q, 4, 0), *single[:2])
        states = [
            cmul(
                jnp.broadcast_to(q_re[d : d + 1], (8, FILT)),
                jnp.broadcast_to(q_im[d : d + 1], (8, FILT)),
                block_re[:, lanes], block_im[:, lanes],
            )
            for d in range(4)
        ]
        s_re, s_im = zip(*states, cmul(q_re, q_im, *single[2:]))
        full = dot3(
            *halves(jnp.concatenate(s_re + s_im, axis=0)),
            *lead_tables(lanes, pr_head, pr_tail, pi_head, pi_tail), 1,
        )
        local, k = (local0, j) if j < EARLY else (local1, j - EARLY)
        f_re = full[0:40, 0:128] - full[40:80, 128:256] + local[k, 0]
        f_im = full[0:40, 128:256] + full[40:80, 0:128] + local[k, 1]
        for c, f in enumerate((f_re, f_im)):
            after = f[32:40] * keep
            for d in range(4):
                own = f[8 * d : 8 * d + 8]
                grouped[c, d, 8 * j : 8 * j + 8, :] = own
                grouped[c, d, 64 + 8 * j : 72 + 8 * j, :] = jnp.where(
                    bottom, after[d : d + 1], pltpu.roll(own, 7, 0)
                )

    for d in range(4):
        ahead = dot3(h_head, h_tail, *halves(delayed(halo[d : d + 1])))
        for c in range(2):
            rows = pl.ds(71, 8, stride=8)
            grouped[c, d, rows, :] = grouped[c, d, rows, :] + ahead[8 * c : 8 * c + 8]

    early = lax.broadcasted_iota(jnp.int32, (64, 128), 1) < 64
    for c in range(2):
        for d in range(4):
            t = grouped[c, d].T
            top, low = t[0:64], t[64:128]
            shifted[c, d, 0:64, :] = jnp.where(early, top, pltpu.roll(low, 64, 1))
            shifted[c, d, 64:128, :] = jnp.where(early, low, top)
            shifted[c, d, 128:192, :] = jnp.where(early, pltpu.roll(top, 64, 1), low)

    def one_sky(s, best):
        total = [None] * 4
        for d in range(4):
            rows = pl.ds(delay[d, s], 64)
            for c in range(2):
                piece = shifted[c, d, rows, :]
                for p in range(2 if d else 1):
                    term = antenna[4 * p + d, s] * piece
                    k = 2 * p + c
                    total[k] = term if total[k] is None else total[k] + term
        energy = (total[0] * total[0] + total[1] * total[1]) + (
            total[2] * total[2] + total[3] * total[3]
        )
        return jnp.maximum(best, energy)

    best = lax.fori_loop(0, SKY, one_sky, jnp.zeros((64, 128), F32), unroll=4)
    turned = best.T
    for j in range(8):
        for m in range(8):
            row = 8 * j + m
            out[j : j + 1, 128 * m : 128 * m + 128] = jnp.concatenate(
                [turned[row : row + 1], turned[64 + row : 65 + row]], axis=1
            )


def call(kernel, n_scalar, n_vector, shapes, scratch, n_unread=0):
    scalar, vector, unread = (
        pl.BlockSpec(memory_space=m) for m in (pltpu.SMEM, pltpu.VMEM, pl.ANY)
    )
    return pl.pallas_call(
        kernel,
        out_shape=[jax.ShapeDtypeStruct(*s) for s in shapes],
        in_specs=[scalar] * n_scalar + [vector] * n_vector + [unread] * n_unread,
        out_specs=[vector] * len(shapes),
        scratch_shapes=[pltpu.VMEM(*s) for s in scratch],
        compiler_params=pltpu.CompilerParams(vmem_limit_bytes=VMEM_LIMIT),
    )


TABLE, EIGHT = ((128, WIDE), BF16), ((8, WIDE), F32)
PREPARED = [TABLE] * 4 + [EIGHT] * 4 + [((32, WIDE), F32)] * 2 + [EIGHT] * 2
PREPARED += [((16, 128), F32), ((8, SKY), F32), ((4, SKY), jnp.int32)]
STATE = ((8, WIDE + 128), F32)


def prepare(*args):
    return call(prepare_kernel, 1, 6, PREPARED, [((4, 16, 128), F32)])(*args)


def of_column(*args):
    scratch = [((512, 128), F32), ((256, 384), BF16)]
    return call(column_kernel, 1, 10, [((2, 8, WIDE + 128), F32)], scratch)(*args)[0]


def of_chip(*args):
    return call(chip_kernel, 1, 4, [STATE] * 4, [], 1)(*args)


def of_device(first, count, *args):
    kernel = functools.partial(local_kernel, first=first)
    return call(kernel, 1, 11, [((count, 2, 40, 128), F32)], [])(*args)[0]


def to_peak(*args):
    scratch = [((2, 4, 128, 128), F32), ((2, 4, 192, 128), F32)]
    return call(peak_kernel, 3, 15, [((8, 1024), F32)], scratch)(*args)[0]


def shards(strain, decay_rate, frequency, gain, member, sky_delay, antenna):
    sent = jnp.broadcast_to(strain.reshape(1, 8, 128), (32, 8, 128))
    column = lax.all_to_all(sent, ("z", "det"), 0, 0, tiled=True).reshape(256, 128)
    plane = 2 * lax.axis_index("x") + lax.axis_index("core")
    place = jnp.stack([lax.axis_index("z"), plane, lax.axis_index("det")]).astype(jnp.int32)
    flip = jnp.asarray(np.eye(128, dtype=np.float32)[::-1], dtype=BF16)
    *tables, rr, ri, br, bi, wr, wi, vr, vi, response, weight, delay = prepare(
        place, decay_rate.reshape(64, 128), frequency.reshape(64, 128), gain, member.reshape(64, 128),
        jnp.transpose(antenna, (1, 2, 0)).reshape(8, SKY), sky_delay.T,
    )
    mine = of_column(place, column, flip, *tables, rr, ri, wr, wi)
    other = lax.ppermute(mine, "core", [(0, 1), (1, 0)])
    of = (place, column, flip, *tables, rr, ri, br, bi, response)
    local0 = of_device(0, EARLY, *of)
    first, *rest = of_chip(place, mine, other, vr, vi, local0)
    got = [
        lax.ppermute(v, "x", [(x, (x + k) % 4) for x in range(4)]) for k, v in enumerate(rest, 1)
    ]
    local1 = of_device(EARLY, 8 - EARLY, *of)
    return to_peak(
        place, delay, weight, first, *got, local0, local1, response, *tables, rr, ri, br, bi
    )


def solution(mesh):
    fine = Mesh(mesh.devices.reshape(8, 4, 2, 4), ("z", "x", "core", "det"))
    time = ("z", "x", "core")
    in_specs = (P("det", time), P(), P(), P(), P(), P(), P())
    return jax.shard_map(
        shards, mesh=fine, in_specs=in_specs, out_specs=P("det", time), check_vma=False
    )
```

```python
import math

import jax
import jax.numpy as jnp
import numpy as np
from jax import lax
from jax.experimental import pallas as pl
from jax.experimental.pallas import tpu as pltpu
from jax.sharding import Mesh, PartitionSpec as P

FILT = 256
SKY = 64
WIDE = 8 * FILT
F32, BF16 = jnp.float32, jnp.bfloat16

TURN = 1.0 / (2.0 * math.pi)
TURN_HEAD = math.floor(TURN * 2**14) / 2**14
TURN_TAIL = TURN - TURN_HEAD

ROW_128, ROW_1024, ROW_8192, ROW_GAIN, ROW_LEAD = 0, 1, 2, 3, 4

VMEM_LIMIT = 16 * 2**20
UNROLL = True


def taylor(first, start, count):
    return [
        first * (-1) ** k * math.pi ** (2 * k + start) / math.factorial(2 * k + start)
        for k in range(count)
    ]


SINE, COSINE = taylor(1.0, 1, 8), taylor(1.0, 0, 9)


def horner(coefficients, square):
    total = jnp.full(square.shape, coefficients[-1], F32)
    for c in coefficients[-2::-1]:
        total = total * square + c
    return total


def cmul(ar, ai, br, bi):
    return ar * br - ai * bi, ar * bi + ai * br


def halves(x):
    head = x.astype(BF16)
    return head, (x - head.astype(F32)).astype(BF16)


def dot(a, b, contract_b=0):
    return lax.dot_general(
        a, b, (((1,), (contract_b,)), ((), ())), preferred_element_type=F32
    )


def dot3(a_head, a_tail, b_head, b_tail, contract_b=0):
    rows = a_head.shape[0]
    both = dot(jnp.concatenate([a_head, a_tail], axis=0), b_head, contract_b)
    return both[:rows] + both[rows:] + dot(a_head, b_tail, contract_b)


def lead_tables(lanes, pr_head, pr_tail, pi_head, pi_tail):
    return (
        jnp.concatenate([pr_head[:, lanes], pi_head[:, lanes]], axis=0),
        jnp.concatenate([pr_tail[:, lanes], pi_tail[:, lanes]], axis=0),
    )


def prepare_kernel(
    place, decay, frequency, gain, member, antenna, sky_delay,
    pr_head, pr_tail, pi_head, pi_tail, row_re, row_im, block_re, block_im, wr, wi, vr, vi, response,
    weight, delay, par,
):
    zi, xc, det = place[0], place[1], place[2]

    delay[...] = sky_delay[...]
    one, two = antenna[0:4, :], antenna[4:8, :]
    scale = jnp.maximum(jnp.abs(one[0:1]), jnp.abs(two[0:1]))
    divisor = jnp.where(scale > 0.0, scale, 1.0)
    a, b = jnp.where(scale > 0.0, one[0:1] / divisor, 1.0), two[0:1] / divisor
    size = jnp.sqrt(a * a + b * b)
    cosine, sine = a / size, b / size
    weight[...] = jnp.concatenate([cosine * one + sine * two, cosine * two - sine * one], axis=0)

    index = [
        member[pl.ds(pl.multiple_of(16 * det + 8 * half, 8), 8), :] for half in range(2)
    ]
    high, low = [v >> 7 for v in index], [v & 127 for v in index]

    def one_row(r, carried):
        lanes = pl.ds(pl.multiple_of(r * 128, 128), 128)
        values = (
            decay[pl.ds(r, 1), :],
            frequency[pl.ds(r, 1), :],
            gain[0:1, lanes],
            gain[1:2, lanes],
        )
        spread = [jnp.broadcast_to(v, (8, 128)) for v in values]
        return tuple(
            jnp.where(
                high[h] == r,
                jnp.take_along_axis(spread[k], low[h], axis=1),
                carried[4 * h + k],
            )
            for h in range(2)
            for k in range(4)
        )

    nothing = jnp.zeros((8, 128), F32)
    found = lax.fori_loop(0, 64, one_row, (nothing,) * 8, unroll=8)
    for h in range(2):
        for k in range(4):
            par[k, 8 * h : 8 * h + 8, :] = found[4 * h + k]

    power = jnp.left_shift(1, lax.broadcasted_iota(jnp.int32, (16, 128), 0)).astype(F32)
    place8 = lax.broadcasted_iota(jnp.int32, (8, 128), 0)
    ahead_z = zi - 1 - (lax.broadcasted_iota(jnp.int32, (32, 128), 0) >> 2)
    core = xc & 1
    ahead_x = jnp.where(place8 == 4, 6 * core, jnp.where(place8 == 0, 7, (2 * place8 - 1 - core) & 7))

    def choose(exponent, rows, re, im):
        out_re = jnp.ones(exponent.shape, F32)
        out_im = jnp.zeros(exponent.shape, F32)
        for bit, row in enumerate(rows):
            new_re, new_im = cmul(out_re, out_im, re[row : row + 1], im[row : row + 1])
            on = (exponent >> bit) & 1 == 1
            out_re = jnp.where(on, new_re, out_re)
            out_im = jnp.where(on, new_im, out_im)
        return out_re, out_im

    def one_chunk(c, _):
        lanes = pl.ds(pl.multiple_of(c * 128, 128), 128)
        f = par[1, pl.ds(c, 1), :]
        f_head = jnp.floor(f * 2048.0) * (1.0 / 2048.0)
        f_tail = f - f_head
        first = power * (f_head * TURN_HEAD)
        second = power * (f_head * TURN_TAIL + f_tail * TURN)
        turn = (first - jnp.floor(first + 0.5)) + (second - jnp.floor(second + 0.5))
        turn = turn - jnp.floor(turn + 0.5)
        square = turn * turn
        sine = turn * horner(SINE, square)
        cosine = horner(COSINE, square)
        size = jnp.exp(-power * par[0, pl.ds(c, 1), :])
        re = size * (1.0 - 2.0 * sine * sine)
        im = size * (2.0 * sine * cosine)
        g_re, g_im = par[2, pl.ds(c, 1), :], par[3, pl.ds(c, 1), :]
        l_re, l_im = cmul(g_re, g_im, re[0:1], im[0:1])
        empty = jnp.zeros((3, 128), F32)
        for single, v, g, lead in ((row_re, re, g_re, l_re), (row_im, im, g_im, l_im)):
            single[:, lanes] = jnp.concatenate(
                [v[7:8], v[10:11], v[13:14], g, lead, empty], axis=0
            )
        block_re[:, lanes], block_im[:, lanes] = choose(place8, (7, 8, 9), re, im)
        w_re, w_im = choose(ahead_z, (13, 14, 15), re, im)
        wr[:, lanes] = jnp.where(ahead_z >= 0, w_re, 0.0)
        wi[:, lanes] = jnp.where(ahead_z >= 0, w_im, 0.0)
        vr[:, lanes], vi[:, lanes] = choose(ahead_x, (10, 11, 12), re, im)
        t_re, t_im = choose(place8, (0, 1, 2), re, im)
        for row in range(3, 7):
            n_re, n_im = cmul(t_re, t_im, re[row : row + 1], im[row : row + 1])
            t_re = jnp.concatenate([t_re, n_re], axis=0)
            t_im = jnp.concatenate([t_im, n_im], axis=0)
        pr_head[:, lanes], pr_tail[:, lanes] = halves(t_re)
        pi_head[:, lanes], pi_tail[:, lanes] = halves(t_im)
        return 0

    lax.fori_loop(0, WIDE // 128, one_chunk, 0)

    for j in range(WIDE // FILT):
        lanes = slice(FILT * j, FILT * j + FILT)
        both_head, both_tail = halves(jnp.concatenate([row_re[:, lanes], row_im[:, lanes]], axis=0))
        full = dot3(both_head, both_tail, *lead_tables(lanes, pr_head, pr_tail, pi_head, pi_tail), 1)
        full_re = full[0:8, 0:128] - full[8:16, 128:256]
        full_im = full[0:8, 128:256] + full[8:16, 0:128]
        response[j : j + 1, :] = full_re[ROW_GAIN : ROW_GAIN + 1]
        response[8 + j : 9 + j, :] = full_im[ROW_GAIN : ROW_GAIN + 1]


def delayed(row):
    lag = lax.broadcasted_iota(jnp.int32, (128, 128), 1) - lax.broadcasted_iota(
        jnp.int32, (128, 128), 0
    )
    rolled = pltpu.roll(jnp.broadcast_to(row, (128, 128)), 0, 1, stride=1, stride_axis=0)
    return jnp.where(lag >= 0, rolled, 0.0)


def column_kernel(
    place, x, flip, pr_head, pr_tail, pi_head, pi_tail, row_re, row_im, wr, wi, vr, vi,
    own_core, other_core, next1, next2, next3, turned, lhs,
):
    zi, xc = place[0], place[1]
    turned[...] = dot(jnp.concatenate(halves(x[...]), axis=0), flip[...])
    for q in range(8):
        rows = [turned[pl.ds(256 * h + 7 - q, 32, stride=8), :].astype(BF16) for h in (0, 1, 0)]
        lhs[32 * q : 32 * q + 32, :] = jnp.concatenate(rows, axis=1)
    own = (lax.broadcasted_iota(jnp.int32, (32, 256), 0) >> 2) == zi
    upper = lax.broadcasted_iota(jnp.int32, (8, 256), 0) < 4

    def over_shards(v):
        total = (v[0:8] + v[8:16]) + (v[16:24] + v[24:32])
        return total + pltpu.roll(total, 4, 0)

    def one_part(part, _):
        lanes = pl.ds(pl.multiple_of(part * 256, 256), 256)
        e_re, e_im = (
            dot(lhs[...], jnp.concatenate([head[:, lanes], head[:, lanes], tail[:, lanes]], axis=0))
            for head, tail in ((pr_head, pr_tail), (pi_head, pi_tail))
        )
        step_re = row_re[ROW_128 : ROW_128 + 1, lanes]
        step_im = row_im[ROW_128 : ROW_128 + 1, lanes]
        s_re, s_im = e_re[224:256], e_im[224:256]
        for q in range(6, -1, -1):
            s_re, s_im = cmul(s_re, s_im, step_re, step_im)
            s_re = s_re + e_re[32 * q : 32 * q + 32]
            s_im = s_im + e_im[32 * q : 32 * q + 32]
        b_re, b_im = (over_shards(v) for v in cmul(s_re, s_im, wr[:, lanes], wi[:, lanes]))
        o_re, o_im = (over_shards(jnp.where(own, v, 0.0)) for v in (s_re, s_im))
        i_re, i_im = cmul(
            b_re, b_im,
            row_re[ROW_8192 : ROW_8192 + 1, lanes], row_im[ROW_8192 : ROW_8192 + 1, lanes],
        )
        before = jnp.where(upper, b_re, b_im)
        through = jnp.where(upper, i_re + o_re, i_im + o_im)
        x_at, core = xc >> 1, xc & 1
        for row, sent in enumerate((own_core, next1, next2, next3, other_core)):
            if row == 0:
                state = before
            elif row == 4:
                state = jnp.where(core == 0, through, before)
            else:
                state = jnp.where(x_at + row < 4, through, before)
            turn = vi[row : row + 1, lanes]
            sent[:, lanes] = state * vr[row : row + 1, lanes] + pltpu.roll(
                state, 4, 0
            ) * jnp.where(upper, -turn, turn)
        return 0

    lax.fori_loop(0, WIDE // 256, one_part, 0, unroll=UNROLL)

    shard = jnp.where(xc == 0, zi + 1, zi)
    inside = shard < 8
    row = jnp.minimum(shard, 7) * 32
    halo = jnp.concatenate(
        [x[pl.ds(row + 8 * d, 1), :] for d in range(4)] + [jnp.zeros((4, 128), F32)],
        axis=0,
    )
    halo = jnp.where(inside, halo, 0.0)
    nothing = jnp.zeros((8, 128), F32)
    for sent, v in ((own_core, nothing), (next1, nothing), (next2, nothing), (next3, halo), (other_core, halo)):
        sent[:, WIDE : WIDE + 128] = v


def local_kernel(
    place, x, flip, pr_head, pr_tail, pi_head, pi_tail, row_re, row_im, block_re, block_im, response,
    local,
):
    zi = place[0]
    n_head, n_tail = halves(x[pl.ds(pl.multiple_of(32 * zi, 32), 32), :])
    x_head, x_tail = (dot(v, flip[...]).astype(BF16) for v in (n_head, n_tail))
    row8 = lax.broadcasted_iota(jnp.int32, (8, FILT), 0)
    for j in range(WIDE // FILT):
        lanes = slice(FILT * j, FILT * j + FILT)
        l_re = dot3(x_head, x_tail, pr_head[:, lanes], pr_tail[:, lanes])
        l_im = dot3(x_head, x_tail, pi_head[:, lanes], pi_tail[:, lanes])
        g_re, g_im = (v[ROW_LEAD : ROW_LEAD + 1, lanes] for v in (row_re, row_im))
        s_re, s_im, end_re, end_im = [], [], [], []
        for d in range(4):
            q_re, q_im = cmul(l_re[8 * d : 8 * d + 8], l_im[8 * d : 8 * d + 8], g_re, g_im)
            for step in (1, 2, 4):
                t_re, t_im = cmul(
                    pltpu.roll(q_re, step, 0), pltpu.roll(q_im, step, 0),
                    block_re[step : step + 1, lanes], block_im[step : step + 1, lanes],
                )
                q_re = q_re + jnp.where(row8 >= step, t_re, 0.0)
                q_im = q_im + jnp.where(row8 >= step, t_im, 0.0)
            s_re.append(jnp.where(row8 >= 1, pltpu.roll(q_re, 1, 0), 0.0))
            s_im.append(jnp.where(row8 >= 1, pltpu.roll(q_im, 1, 0), 0.0))
            end_re.append(q_re[7:8])
            end_im.append(q_im[7:8])
        none = [jnp.zeros((4, FILT), F32)]
        full = dot3(
            *halves(jnp.concatenate(s_re + end_re + none + s_im + end_im + none, axis=0)),
            *lead_tables(lanes, pr_head, pr_tail, pi_head, pi_tail), 1,
        )
        matrices = [delayed(response[row : row + 1, :]) for row in (j, 8 + j)]
        own = dot3(n_head, n_tail, *halves(jnp.concatenate(matrices, axis=1)))
        f_re = full[0:40, 0:128] - full[40:80, 128:256]
        f_im = full[0:40, 128:256] + full[40:80, 0:128]
        local[j, 0, 0:32, :], local[j, 0, 32:40, :] = f_re[0:32] + own[:, 0:128], f_re[32:40]
        local[j, 1, 0:32, :], local[j, 1, 32:40, :] = f_im[0:32] + own[:, 128:256], f_im[32:40]


def peak_kernel(
    place, delay, antenna, own_core, other_core, own_sum, other_sum, local, response,
    pr_head, pr_tail, pi_head, pi_tail, row_re, row_im, block_re, block_im,
    out, grouped, shifted,
):
    zi, xc = place[0], place[1]
    keep = jnp.where(jnp.logical_and(zi == 7, xc == 7), 0.0, 1.0)
    ahead_lanes = slice(WIDE, WIDE + 128)
    second = (xc & 1) == 1
    halo = jnp.where(second, other_sum[:, ahead_lanes], other_core[:, ahead_lanes])
    h_head, h_tail = halves(response[...])
    bottom = lax.broadcasted_iota(jnp.int32, (8, 128), 0) == 7

    for j in range(WIDE // FILT):
        lanes = slice(FILT * j, FILT * j + FILT)
        single = [
            v[row : row + 1, lanes] for row in (ROW_LEAD, ROW_1024) for v in (row_re, row_im)
        ]
        q = own_sum[:, lanes] + other_sum[:, lanes]
        q_re, q_im = cmul(
            q, pltpu.roll(q, 4, 0),
            jnp.where(second, single[2], 1.0), jnp.where(second, single[3], 0.0),
        )
        q = own_core[:, lanes] + other_core[:, lanes]
        q_re, q_im = cmul(q_re + q, q_im + pltpu.roll(q, 4, 0), *single[:2])
        states = [
            cmul(
                jnp.broadcast_to(q_re[d : d + 1], (8, FILT)),
                jnp.broadcast_to(q_im[d : d + 1], (8, FILT)),
                block_re[:, lanes], block_im[:, lanes],
            )
            for d in range(4)
        ]
        s_re, s_im = zip(*states, cmul(q_re, q_im, *single[2:]))
        full = dot3(
            *halves(jnp.concatenate(s_re + s_im, axis=0)),
            *lead_tables(lanes, pr_head, pr_tail, pi_head, pi_tail), 1,
        )
        f_re = full[0:40, 0:128] - full[40:80, 128:256] + local[j, 0]
        f_im = full[0:40, 128:256] + full[40:80, 0:128] + local[j, 1]
        for c, f in enumerate((f_re, f_im)):
            after = f[32:40] * keep
            for d in range(4):
                own = f[8 * d : 8 * d + 8]
                grouped[c, d, 8 * j : 8 * j + 8, :] = own
                grouped[c, d, 64 + 8 * j : 72 + 8 * j, :] = jnp.where(
                    bottom, after[d : d + 1], pltpu.roll(own, 7, 0)
                )

    for d in range(4):
        ahead = dot3(h_head, h_tail, *halves(delayed(halo[d : d + 1])))
        for c in range(2):
            rows = pl.ds(71, 8, stride=8)
            grouped[c, d, rows, :] = grouped[c, d, rows, :] + ahead[8 * c : 8 * c + 8]

    early = lax.broadcasted_iota(jnp.int32, (64, 128), 1) < 64
    for c in range(2):
        for d in range(4):
            t = grouped[c, d].T
            top, low = t[0:64], t[64:128]
            shifted[c, d, 0:64, :] = jnp.where(early, top, pltpu.roll(low, 64, 1))
            shifted[c, d, 64:128, :] = jnp.where(early, low, top)
            shifted[c, d, 128:192, :] = jnp.where(early, pltpu.roll(top, 64, 1), low)

    def one_sky(s, best):
        total = [None] * 4
        for d in range(4):
            rows = pl.ds(delay[d, s], 64)
            for c in range(2):
                piece = shifted[c, d, rows, :]
                for p in range(2 if d else 1):
                    term = antenna[4 * p + d, s] * piece
                    k = 2 * p + c
                    total[k] = term if total[k] is None else total[k] + term
        energy = (total[0] * total[0] + total[1] * total[1]) + (
            total[2] * total[2] + total[3] * total[3]
        )
        return jnp.maximum(best, energy)

    best = lax.fori_loop(0, SKY, one_sky, jnp.zeros((64, 128), F32), unroll=4)
    turned = best.T
    for j in range(8):
        for m in range(8):
            row = 8 * j + m
            out[j : j + 1, 128 * m : 128 * m + 128] = jnp.concatenate(
                [turned[row : row + 1], turned[64 + row : 65 + row]], axis=1
            )


def call(kernel, n_scalar, n_vector, shapes, scratch):
    scalar, vector = (pl.BlockSpec(memory_space=m) for m in (pltpu.SMEM, pltpu.VMEM))
    return pl.pallas_call(
        kernel,
        out_shape=[jax.ShapeDtypeStruct(*s) for s in shapes],
        in_specs=[scalar] * n_scalar + [vector] * n_vector,
        out_specs=[vector] * len(shapes),
        scratch_shapes=[pltpu.VMEM(*s) for s in scratch],
        compiler_params=pltpu.CompilerParams(vmem_limit_bytes=VMEM_LIMIT),
    )


TABLE, EIGHT = ((128, WIDE), BF16), ((8, WIDE), F32)
PREPARED = [TABLE] * 4 + [EIGHT] * 4 + [((32, WIDE), F32)] * 2 + [EIGHT] * 2
PREPARED += [((16, 128), F32), ((8, SKY), F32), ((4, SKY), jnp.int32)]
STATE = ((8, WIDE + 128), F32)


def prepare(*args):
    return call(prepare_kernel, 1, 6, PREPARED, [((4, 16, 128), F32)])(*args)


def of_column(*args):
    scratch = [((512, 128), F32), ((256, 384), BF16)]
    return call(column_kernel, 1, 12, [STATE] * 5, scratch)(*args)


def of_device(*args):
    return call(local_kernel, 1, 11, [((8, 2, 40, 128), F32)], [])(*args)[0]


def to_peak(*args):
    scratch = [((2, 4, 128, 128), F32), ((2, 4, 192, 128), F32)]
    return call(peak_kernel, 3, 14, [((8, 1024), F32)], scratch)(*args)[0]


def shards(strain, decay_rate, frequency, gain, member, sky_delay, antenna):
    sent = jnp.broadcast_to(strain.reshape(1, 8, 128), (32, 8, 128))
    column = lax.all_to_all(sent, ("z", "det"), 0, 0, tiled=True).reshape(256, 128)
    plane = 2 * lax.axis_index("x") + lax.axis_index("core")
    place = jnp.stack([lax.axis_index("z"), plane, lax.axis_index("det")]).astype(jnp.int32)
    flip = jnp.asarray(np.eye(128, dtype=np.float32)[::-1], dtype=BF16)
    *tables, rr, ri, br, bi, wr, wi, vr, vi, response, weight, delay = prepare(
        place, decay_rate.reshape(64, 128), frequency.reshape(64, 128), gain, member.reshape(64, 128),
        jnp.transpose(antenna, (1, 2, 0)).reshape(8, SKY), sky_delay.T,
    )
    own_core, other_core, *following = of_column(
        place, column, flip, *tables, rr, ri, wr, wi, vr, vi
    )
    got = [
        lax.ppermute(v, "x", [(x, (x + k) % 4) for x in range(4)])
        for k, v in enumerate(following, 1)
    ]
    local = of_device(place, column, flip, *tables, rr, ri, br, bi, response)
    *got, local = lax.optimization_barrier((*got, local))
    own_sum = got[0] + got[1] + got[2]
    swap = [(0, 1), (1, 0)]
    return to_peak(
        place, delay, weight, own_core, lax.ppermute(other_core, "core", swap),
        own_sum, lax.ppermute(own_sum, "core", swap), local, response, *tables, rr, ri, br, bi,
    )


def solution(mesh):
    fine = Mesh(mesh.devices.reshape(8, 4, 2, 4), ("z", "x", "core", "det"))
    time = ("z", "x", "core")
    in_specs = (P("det", time), P(), P(), P(), P(), P(), P())
    return jax.shard_map(
        shards, mesh=fine, in_specs=in_specs, out_specs=P("det", time), check_vma=False
    )
```

```python
import math

import jax
import jax.numpy as jnp
import numpy as np
from jax import lax
from jax.experimental import pallas as pl
from jax.experimental.pallas import tpu as pltpu
from jax.sharding import Mesh, PartitionSpec as P

FILT = 256
SKY = 64
WIDE = 8 * FILT
F32, BF16 = jnp.float32, jnp.bfloat16

TURN = 1.0 / (2.0 * math.pi)
TURN_HEAD = math.floor(TURN * 2**14) / 2**14
TURN_TAIL = TURN - TURN_HEAD

ROW_128, ROW_1024, ROW_8192, ROW_GAIN, ROW_LEAD = 0, 1, 2, 3, 4

VMEM_LIMIT = 16 * 2**20


def taylor(first, start, count):
    return [
        first * (-1) ** k * math.pi ** (2 * k + start) / math.factorial(2 * k + start)
        for k in range(count)
    ]


SINE, COSINE = taylor(1.0, 1, 8), taylor(1.0, 0, 9)


def horner(coefficients, square):
    total = jnp.full(square.shape, coefficients[-1], F32)
    for c in coefficients[-2::-1]:
        total = total * square + c
    return total


def cmul(ar, ai, br, bi):
    return ar * br - ai * bi, ar * bi + ai * br


def halves(x):
    head = x.astype(BF16)
    return head, (x - head.astype(F32)).astype(BF16)


def dot(a, b, contract_b=0):
    return lax.dot_general(
        a, b, (((1,), (contract_b,)), ((), ())), preferred_element_type=F32
    )


def dot3(a_head, a_tail, b_head, b_tail, contract_b=0):
    rows = a_head.shape[0]
    both = dot(jnp.concatenate([a_head, a_tail], axis=0), b_head, contract_b)
    return both[:rows] + both[rows:] + dot(a_head, b_tail, contract_b)


def lead_tables(lanes, pr_head, pr_tail, pi_head, pi_tail):
    return (
        jnp.concatenate([pr_head[:, lanes], pi_head[:, lanes]], axis=0),
        jnp.concatenate([pr_tail[:, lanes], pi_tail[:, lanes]], axis=0),
    )


def prepare_kernel(
    place, decay, frequency, gain, member, antenna, sky_delay,
    pr_head, pr_tail, pi_head, pi_tail, row_re, row_im, block_re, block_im, wr, wi, vr, vi, response,
    weight, delay, par,
):
    zi, xc, det = place[0], place[1], place[2]

    delay[...] = sky_delay[...]
    one, two = antenna[0:4, :], antenna[4:8, :]
    scale = jnp.maximum(jnp.abs(one[0:1]), jnp.abs(two[0:1]))
    divisor = jnp.where(scale > 0.0, scale, 1.0)
    a, b = jnp.where(scale > 0.0, one[0:1] / divisor, 1.0), two[0:1] / divisor
    size = jnp.sqrt(a * a + b * b)
    cosine, sine = a / size, b / size
    weight[...] = jnp.concatenate([cosine * one + sine * two, cosine * two - sine * one], axis=0)

    index = [
        member[pl.ds(pl.multiple_of(16 * det + 8 * half, 8), 8), :] for half in range(2)
    ]
    high, low = [v >> 7 for v in index], [v & 127 for v in index]

    def one_row(r, carried):
        lanes = pl.ds(pl.multiple_of(r * 128, 128), 128)
        values = (
            decay[pl.ds(r, 1), :],
            frequency[pl.ds(r, 1), :],
            gain[0:1, lanes],
            gain[1:2, lanes],
        )
        spread = [jnp.broadcast_to(v, (8, 128)) for v in values]
        return tuple(
            jnp.where(
                high[h] == r,
                jnp.take_along_axis(spread[k], low[h], axis=1),
                carried[4 * h + k],
            )
            for h in range(2)
            for k in range(4)
        )

    nothing = jnp.zeros((8, 128), F32)
    found = lax.fori_loop(0, 64, one_row, (nothing,) * 8, unroll=8)
    for h in range(2):
        for k in range(4):
            par[k, 8 * h : 8 * h + 8, :] = found[4 * h + k]

    power = jnp.left_shift(1, lax.broadcasted_iota(jnp.int32, (16, 128), 0)).astype(F32)
    place8 = lax.broadcasted_iota(jnp.int32, (8, 128), 0)
    ahead_z = zi - 1 - (lax.broadcasted_iota(jnp.int32, (32, 128), 0) >> 2)
    core = xc & 1
    ahead_x = jnp.where(place8 == 4, 6 * core, jnp.where(place8 == 0, 7, (2 * place8 - 1 - core) & 7))

    def choose(exponent, rows, re, im):
        out_re = jnp.ones(exponent.shape, F32)
        out_im = jnp.zeros(exponent.shape, F32)
        for bit, row in enumerate(rows):
            new_re, new_im = cmul(out_re, out_im, re[row : row + 1], im[row : row + 1])
            on = (exponent >> bit) & 1 == 1
            out_re = jnp.where(on, new_re, out_re)
            out_im = jnp.where(on, new_im, out_im)
        return out_re, out_im

    def one_chunk(c, _):
        lanes = pl.ds(pl.multiple_of(c * 128, 128), 128)
        f = par[1, pl.ds(c, 1), :]
        f_head = jnp.floor(f * 2048.0) * (1.0 / 2048.0)
        f_tail = f - f_head
        first = power * (f_head * TURN_HEAD)
        second = power * (f_head * TURN_TAIL + f_tail * TURN)
        turn = (first - jnp.floor(first + 0.5)) + (second - jnp.floor(second + 0.5))
        turn = turn - jnp.floor(turn + 0.5)
        square = turn * turn
        sine = turn * horner(SINE, square)
        cosine = horner(COSINE, square)
        size = jnp.exp(-power * par[0, pl.ds(c, 1), :])
        re = size * (1.0 - 2.0 * sine * sine)
        im = size * (2.0 * sine * cosine)
        g_re, g_im = par[2, pl.ds(c, 1), :], par[3, pl.ds(c, 1), :]
        l_re, l_im = cmul(g_re, g_im, re[0:1], im[0:1])
        empty = jnp.zeros((3, 128), F32)
        for single, v, g, lead in ((row_re, re, g_re, l_re), (row_im, im, g_im, l_im)):
            single[:, lanes] = jnp.concatenate(
                [v[7:8], v[10:11], v[13:14], g, lead, empty], axis=0
            )
        block_re[:, lanes], block_im[:, lanes] = choose(place8, (7, 8, 9), re, im)
        w_re, w_im = choose(ahead_z, (13, 14, 15), re, im)
        wr[:, lanes] = jnp.where(ahead_z >= 0, w_re, 0.0)
        wi[:, lanes] = jnp.where(ahead_z >= 0, w_im, 0.0)
        vr[:, lanes], vi[:, lanes] = choose(ahead_x, (10, 11, 12), re, im)
        t_re, t_im = choose(place8, (0, 1, 2), re, im)
        for row in range(3, 7):
            n_re, n_im = cmul(t_re, t_im, re[row : row + 1], im[row : row + 1])
            t_re = jnp.concatenate([t_re, n_re], axis=0)
            t_im = jnp.concatenate([t_im, n_im], axis=0)
        pr_head[:, lanes], pr_tail[:, lanes] = halves(t_re)
        pi_head[:, lanes], pi_tail[:, lanes] = halves(t_im)
        return 0

    lax.fori_loop(0, WIDE // 128, one_chunk, 0, unroll=4)

    for j in range(WIDE // FILT):
        lanes = slice(FILT * j, FILT * j + FILT)
        both_head, both_tail = halves(jnp.concatenate([row_re[:, lanes], row_im[:, lanes]], axis=0))
        full = dot3(both_head, both_tail, *lead_tables(lanes, pr_head, pr_tail, pi_head, pi_tail), 1)
        full_re = full[0:8, 0:128] - full[8:16, 128:256]
        full_im = full[0:8, 128:256] + full[8:16, 0:128]
        response[j : j + 1, :] = full_re[ROW_GAIN : ROW_GAIN + 1]
        response[8 + j : 9 + j, :] = full_im[ROW_GAIN : ROW_GAIN + 1]


def delayed(row):
    lag = lax.broadcasted_iota(jnp.int32, (128, 128), 1) - lax.broadcasted_iota(
        jnp.int32, (128, 128), 0
    )
    rolled = pltpu.roll(jnp.broadcast_to(row, (128, 128)), 0, 1, stride=1, stride_axis=0)
    return jnp.where(lag >= 0, rolled, 0.0)


def column_kernel(
    place, x, flip, pr_head, pr_tail, pi_head, pi_tail, row_re, row_im, wr, wi, vr, vi,
    own_core, other_core, next1, next2, next3, turned, lhs, total,
):
    zi, xc = place[0], place[1]
    turned[0:512, :] = dot(jnp.concatenate(halves(x[...]), axis=0), flip[...])
    for half in range(2):
        for q in range(8):
            rows = [
                turned[pl.ds(256 * h + 128 * half + 7 - q, 16, stride=8), :].astype(BF16)
                for h in (0, 1, 0)
            ]
            at = 128 * half + 16 * q
            lhs[at : at + 16, :] = jnp.concatenate(rows, axis=1)
    shard_of = lax.broadcasted_iota(jnp.int32, (16, 256), 0) >> 2
    upper = lax.broadcasted_iota(jnp.int32, (8, 256), 0) < 4
    x_at, core = xc >> 1, xc & 1

    def over_shards(v):
        total = v[0:8] + v[8:16]
        return total + pltpu.roll(total, 4, 0)

    def of_half(half, lanes):
        e_re, e_im = (
            dot(
                lhs[128 * half : 128 * half + 128, :],
                jnp.concatenate([head[:, lanes], head[:, lanes], tail[:, lanes]], axis=0),
            )
            for head, tail in ((pr_head, pr_tail), (pi_head, pi_tail))
        )
        step_re = row_re[ROW_128 : ROW_128 + 1, lanes]
        step_im = row_im[ROW_128 : ROW_128 + 1, lanes]
        s_re, s_im = e_re[112:128], e_im[112:128]
        for q in range(6, -1, -1):
            s_re, s_im = cmul(s_re, s_im, step_re, step_im)
            s_re = s_re + e_re[16 * q : 16 * q + 16]
            s_im = s_im + e_im[16 * q : 16 * q + 16]
        rows = slice(16 * half, 16 * half + 16)
        weighted = cmul(s_re, s_im, wr[rows, lanes], wi[rows, lanes])
        own = [jnp.where(shard_of == zi - 4 * half, v, 0.0) for v in (s_re, s_im)]
        return [over_shards(v) for v in (*weighted, *own)]

    parts = [slice(256 * part, 256 * part + 256) for part in range(WIDE // 256)]
    for lanes in parts:
        for k, v in enumerate(of_half(0, lanes)):
            total[k, :, lanes] = v

    @pl.when(zi >= 4)
    def _():
        for lanes in parts:
            for k, v in enumerate(of_half(1, lanes)):
                total[k, :, lanes] = total[k, :, lanes] + v

    for lanes in parts:
        b_re, b_im, o_re, o_im = (total[k, :, lanes] for k in range(4))
        i_re, i_im = cmul(
            b_re, b_im,
            row_re[ROW_8192 : ROW_8192 + 1, lanes], row_im[ROW_8192 : ROW_8192 + 1, lanes],
        )
        before = jnp.where(upper, b_re, b_im)
        through = jnp.where(upper, i_re + o_re, i_im + o_im)
        for row, sent in enumerate((own_core, next1, next2, next3, other_core)):
            if row == 0:
                state = before
            elif row == 4:
                state = jnp.where(core == 0, through, before)
            else:
                state = jnp.where(x_at + row < 4, through, before)
            turn = vi[row : row + 1, lanes]
            sent[:, lanes] = state * vr[row : row + 1, lanes] + pltpu.roll(
                state, 4, 0
            ) * jnp.where(upper, -turn, turn)

    shard = jnp.where(xc == 0, zi + 1, zi)
    inside = shard < 8
    row = jnp.minimum(shard, 7) * 32
    halo = jnp.concatenate(
        [x[pl.ds(row + 8 * d, 1), :] for d in range(4)] + [jnp.zeros((4, 128), F32)],
        axis=0,
    )
    halo = jnp.where(inside, halo, 0.0)
    nothing = jnp.zeros((8, 128), F32)
    for sent, v in ((own_core, nothing), (next1, nothing), (next2, nothing), (next3, halo), (other_core, halo)):
        sent[:, WIDE : WIDE + 128] = v


def local_kernel(
    place, x, flip, pr_head, pr_tail, pi_head, pi_tail, row_re, row_im, block_re, block_im, response,
    local,
):
    zi = place[0]
    n_head, n_tail = halves(x[pl.ds(pl.multiple_of(32 * zi, 32), 32), :])
    x_head, x_tail = (dot(v, flip[...]).astype(BF16) for v in (n_head, n_tail))
    row8 = lax.broadcasted_iota(jnp.int32, (8, FILT), 0)
    for j in range(WIDE // FILT):
        lanes = slice(FILT * j, FILT * j + FILT)
        l_re = dot3(x_head, x_tail, pr_head[:, lanes], pr_tail[:, lanes])
        l_im = dot3(x_head, x_tail, pi_head[:, lanes], pi_tail[:, lanes])
        g_re, g_im = (v[ROW_LEAD : ROW_LEAD + 1, lanes] for v in (row_re, row_im))
        s_re, s_im, end_re, end_im = [], [], [], []
        for d in range(4):
            q_re, q_im = cmul(l_re[8 * d : 8 * d + 8], l_im[8 * d : 8 * d + 8], g_re, g_im)
            for step in (1, 2, 4):
                t_re, t_im = cmul(
                    pltpu.roll(q_re, step, 0), pltpu.roll(q_im, step, 0),
                    block_re[step : step + 1, lanes], block_im[step : step + 1, lanes],
                )
                q_re = q_re + jnp.where(row8 >= step, t_re, 0.0)
                q_im = q_im + jnp.where(row8 >= step, t_im, 0.0)
            s_re.append(jnp.where(row8 >= 1, pltpu.roll(q_re, 1, 0), 0.0))
            s_im.append(jnp.where(row8 >= 1, pltpu.roll(q_im, 1, 0), 0.0))
            end_re.append(q_re[7:8])
            end_im.append(q_im[7:8])
        none = [jnp.zeros((4, FILT), F32)]
        full = dot3(
            *halves(jnp.concatenate(s_re + end_re + none + s_im + end_im + none, axis=0)),
            *lead_tables(lanes, pr_head, pr_tail, pi_head, pi_tail), 1,
        )
        matrices = [delayed(response[row : row + 1, :]) for row in (j, 8 + j)]
        own = dot3(n_head, n_tail, *halves(jnp.concatenate(matrices, axis=1)))
        f_re = full[0:40, 0:128] - full[40:80, 128:256]
        f_im = full[0:40, 128:256] + full[40:80, 0:128]
        local[j, 0, 0:32, :], local[j, 0, 32:40, :] = f_re[0:32] + own[:, 0:128], f_re[32:40]
        local[j, 1, 0:32, :], local[j, 1, 32:40, :] = f_im[0:32] + own[:, 128:256], f_im[32:40]


def peak_kernel(
    place, delay, antenna, own_core, other_core, own_sum, other_sum, local, response,
    pr_head, pr_tail, pi_head, pi_tail, row_re, row_im, block_re, block_im,
    out, grouped, shifted,
):
    zi, xc = place[0], place[1]
    keep = jnp.where(jnp.logical_and(zi == 7, xc == 7), 0.0, 1.0)
    ahead_lanes = slice(WIDE, WIDE + 128)
    second = (xc & 1) == 1
    halo = jnp.where(second, other_sum[:, ahead_lanes], other_core[:, ahead_lanes])
    h_head, h_tail = halves(response[...])
    bottom = lax.broadcasted_iota(jnp.int32, (8, 128), 0) == 7

    for j in range(WIDE // FILT):
        lanes = slice(FILT * j, FILT * j + FILT)
        single = [
            v[row : row + 1, lanes] for row in (ROW_LEAD, ROW_1024) for v in (row_re, row_im)
        ]
        q = own_sum[:, lanes] + other_sum[:, lanes]
        q_re, q_im = cmul(
            q, pltpu.roll(q, 4, 0),
            jnp.where(second, single[2], 1.0), jnp.where(second, single[3], 0.0),
        )
        q = own_core[:, lanes] + other_core[:, lanes]
        q_re, q_im = cmul(q_re + q, q_im + pltpu.roll(q, 4, 0), *single[:2])
        states = [
            cmul(
                jnp.broadcast_to(q_re[d : d + 1], (8, FILT)),
                jnp.broadcast_to(q_im[d : d + 1], (8, FILT)),
                block_re[:, lanes], block_im[:, lanes],
            )
            for d in range(4)
        ]
        s_re, s_im = zip(*states, cmul(q_re, q_im, *single[2:]))
        full = dot3(
            *halves(jnp.concatenate(s_re + s_im, axis=0)),
            *lead_tables(lanes, pr_head, pr_tail, pi_head, pi_tail), 1,
        )
        f_re = full[0:40, 0:128] - full[40:80, 128:256] + local[j, 0]
        f_im = full[0:40, 128:256] + full[40:80, 0:128] + local[j, 1]
        for c, f in enumerate((f_re, f_im)):
            after = f[32:40] * keep
            for d in range(4):
                own = f[8 * d : 8 * d + 8]
                grouped[c, d, 8 * j : 8 * j + 8, :] = own
                grouped[c, d, 64 + 8 * j : 72 + 8 * j, :] = jnp.where(
                    bottom, after[d : d + 1], pltpu.roll(own, 7, 0)
                )

    for d in range(4):
        ahead = dot3(h_head, h_tail, *halves(delayed(halo[d : d + 1])))
        for c in range(2):
            rows = pl.ds(71, 8, stride=8)
            grouped[c, d, rows, :] = grouped[c, d, rows, :] + ahead[8 * c : 8 * c + 8]

    early = lax.broadcasted_iota(jnp.int32, (64, 128), 1) < 64
    for c in range(2):
        for d in range(4):
            t = grouped[c, d, 0:128, :].T
            top, low = t[0:64], t[64:128]
            shifted[c, d, 0:64, :] = jnp.where(early, top, pltpu.roll(low, 64, 1))
            shifted[c, d, 64:128, :] = jnp.where(early, low, top)
            shifted[c, d, 128:192, :] = jnp.where(early, pltpu.roll(top, 64, 1), low)

    def one_sky(s, best):
        total = [None] * 4
        for d in range(4):
            rows = pl.ds(delay[d, s], 64)
            for c in range(2):
                piece = shifted[c, d, rows, :]
                for p in range(2 if d else 1):
                    term = antenna[4 * p + d, s] * piece
                    k = 2 * p + c
                    total[k] = term if total[k] is None else total[k] + term
        energy = (total[0] * total[0] + total[1] * total[1]) + (
            total[2] * total[2] + total[3] * total[3]
        )
        return jnp.maximum(best, energy)

    best = lax.fori_loop(0, SKY, one_sky, jnp.zeros((64, 128), F32), unroll=4)
    turned = best.T
    for j in range(8):
        for m in range(8):
            row = 8 * j + m
            out[j : j + 1, 128 * m : 128 * m + 128] = jnp.concatenate(
                [turned[row : row + 1], turned[64 + row : 65 + row]], axis=1
            )


def call(kernel, n_scalar, n_vector, shapes, scratch):
    scalar, vector = (pl.BlockSpec(memory_space=m) for m in (pltpu.SMEM, pltpu.VMEM))
    return pl.pallas_call(
        kernel,
        out_shape=[jax.ShapeDtypeStruct(*s) for s in shapes],
        in_specs=[scalar] * n_scalar + [vector] * n_vector,
        out_specs=[vector] * len(shapes),
        scratch_shapes=[pltpu.VMEM(*s) for s in scratch],
        compiler_params=pltpu.CompilerParams(vmem_limit_bytes=VMEM_LIMIT),
    )


TABLE, EIGHT = ((128, WIDE), BF16), ((8, WIDE), F32)
PREPARED = [TABLE] * 4 + [EIGHT] * 4 + [((32, WIDE), F32)] * 2 + [EIGHT] * 2
PREPARED += [((16, 128), F32), ((8, SKY), F32), ((4, SKY), jnp.int32)]
STATE = ((8, WIDE + 128), F32)


def prepare(*args):
    return call(prepare_kernel, 1, 6, PREPARED, [((4, 16, 128), F32)])(*args)


def of_column(*args):
    scratch = [((520, 128), F32), ((256, 384), BF16), ((4, 8, WIDE), F32)]
    return call(column_kernel, 1, 12, [STATE] * 5, scratch)(*args)


def of_device(*args):
    return call(local_kernel, 1, 11, [((8, 2, 40, 128), F32)], [])(*args)[0]


def to_peak(*args):
    scratch = [((2, 4, 136, 128), F32), ((2, 4, 192, 128), F32)]
    return call(peak_kernel, 3, 14, [((8, 1024), F32)], scratch)(*args)[0]


def shards(strain, decay_rate, frequency, gain, member, sky_delay, antenna):
    sent = jnp.broadcast_to(strain.reshape(1, 8, 128), (32, 8, 128))
    column = lax.all_to_all(sent, ("z", "det"), 0, 0, tiled=True).reshape(256, 128)
    plane = 2 * lax.axis_index("x") + lax.axis_index("core")
    place = jnp.stack([lax.axis_index("z"), plane, lax.axis_index("det")]).astype(jnp.int32)
    flip = jnp.asarray(np.eye(128, dtype=np.float32)[::-1], dtype=BF16)
    *tables, rr, ri, br, bi, wr, wi, vr, vi, response, weight, delay = prepare(
        place, decay_rate.reshape(64, 128), frequency.reshape(64, 128), gain, member.reshape(64, 128),
        jnp.transpose(antenna, (1, 2, 0)).reshape(8, SKY), sky_delay.T,
    )
    own_core, other_core, *following = of_column(
        place, column, flip, *tables, rr, ri, wr, wi, vr, vi
    )
    got = [
        lax.ppermute(v, "x", [(x, (x + k) % 4) for x in range(4)])
        for k, v in enumerate(following, 1)
    ]
    local = of_device(place, column, flip, *tables, rr, ri, br, bi, response)
    *got, local = lax.optimization_barrier((*got, local))
    own_sum = got[0] + got[1] + got[2]
    swap = [(0, 1), (1, 0)]
    return to_peak(
        place, delay, weight, own_core, lax.ppermute(other_core, "core", swap),
        own_sum, lax.ppermute(own_sum, "core", swap), local, response, *tables, rr, ri, br, bi,
    )


def solution(mesh):
    fine = Mesh(mesh.devices.reshape(8, 4, 2, 4), ("z", "x", "core", "det"))
    time = ("z", "x", "core")
    in_specs = (P("det", time), P(), P(), P(), P(), P(), P())
    return jax.shard_map(
        shards, mesh=fine, in_specs=in_specs, out_specs=P("det", time), check_vma=False
    )
```

```python
import math

import jax
import jax.numpy as jnp
import numpy as np
from jax import lax
from jax.experimental import pallas as pl
from jax.experimental.pallas import tpu as pltpu
from jax.sharding import Mesh, PartitionSpec as P

FILT = 256
SKY = 64
WIDE = 8 * FILT
F32, BF16 = jnp.float32, jnp.bfloat16

TURN = 1.0 / (2.0 * math.pi)
TURN_HEAD = math.floor(TURN * 2**14) / 2**14
TURN_TAIL = TURN - TURN_HEAD

ROW_128, ROW_1024, ROW_8192, ROW_GAIN, ROW_LEAD = 0, 1, 2, 3, 4

VMEM_LIMIT = 16 * 2**20


def taylor(first, start, count):
    return [
        first * (-1) ** k * math.pi ** (2 * k + start) / math.factorial(2 * k + start)
        for k in range(count)
    ]


SINE, COSINE = taylor(1.0, 1, 8), taylor(1.0, 0, 9)


def horner(coefficients, square):
    total = jnp.full(square.shape, coefficients[-1], F32)
    for c in coefficients[-2::-1]:
        total = total * square + c
    return total


def cmul(ar, ai, br, bi):
    return ar * br - ai * bi, ar * bi + ai * br


def halves(x):
    head = x.astype(BF16)
    return head, (x - head.astype(F32)).astype(BF16)


def dot(a, b, contract_b=0):
    return lax.dot_general(
        a, b, (((1,), (contract_b,)), ((), ())), preferred_element_type=F32
    )


def dot3(a_head, a_tail, b_head, b_tail, contract_b=0):
    rows = a_head.shape[0]
    both = dot(jnp.concatenate([a_head, a_tail], axis=0), b_head, contract_b)
    return both[:rows] + both[rows:] + dot(a_head, b_tail, contract_b)


def lead_tables(lanes, pr_head, pr_tail, pi_head, pi_tail):
    return (
        jnp.concatenate([pr_head[:, lanes], pi_head[:, lanes]], axis=0),
        jnp.concatenate([pr_tail[:, lanes], pi_tail[:, lanes]], axis=0),
    )


def prepare_kernel(
    place, decay, frequency, gain, member, antenna, sky_delay,
    pr_head, pr_tail, pi_head, pi_tail, row_re, row_im, block_re, block_im, wr, wi, vr, vi, response,
    weight, delay, par,
):
    zi, xc, det = place[0], place[1], place[2]

    delay[...] = sky_delay[...]
    one, two = antenna[0:4, :], antenna[4:8, :]
    scale = jnp.maximum(jnp.abs(one[0:1]), jnp.abs(two[0:1]))
    divisor = jnp.where(scale > 0.0, scale, 1.0)
    a, b = jnp.where(scale > 0.0, one[0:1] / divisor, 1.0), two[0:1] / divisor
    size = jnp.sqrt(a * a + b * b)
    cosine, sine = a / size, b / size
    weight[...] = jnp.concatenate([cosine * one + sine * two, cosine * two - sine * one], axis=0)

    index = [
        member[pl.ds(pl.multiple_of(16 * det + 8 * half, 8), 8), :] for half in range(2)
    ]
    high, low = [v >> 7 for v in index], [v & 127 for v in index]

    def one_row(r, carried):
        lanes = pl.ds(pl.multiple_of(r * 128, 128), 128)
        values = (
            decay[pl.ds(r, 1), :],
            frequency[pl.ds(r, 1), :],
            gain[0:1, lanes],
            gain[1:2, lanes],
        )
        spread = [jnp.broadcast_to(v, (8, 128)) for v in values]
        return tuple(
            jnp.where(
                high[h] == r,
                jnp.take_along_axis(spread[k], low[h], axis=1),
                carried[4 * h + k],
            )
            for h in range(2)
            for k in range(4)
        )

    nothing = jnp.zeros((8, 128), F32)
    found = lax.fori_loop(0, 64, one_row, (nothing,) * 8, unroll=8)
    for h in range(2):
        for k in range(4):
            par[k, 8 * h : 8 * h + 8, :] = found[4 * h + k]

    power = jnp.left_shift(1, lax.broadcasted_iota(jnp.int32, (16, 128), 0)).astype(F32)
    place8 = lax.broadcasted_iota(jnp.int32, (8, 128), 0)
    ahead_z = zi - 1 - (lax.broadcasted_iota(jnp.int32, (32, 128), 0) >> 2)
    core = xc & 1
    ahead_x = jnp.where(place8 == 4, 6 * core, jnp.where(place8 == 0, 7, (2 * place8 - 1 - core) & 7))

    def choose(exponent, rows, re, im):
        out_re = jnp.ones(exponent.shape, F32)
        out_im = jnp.zeros(exponent.shape, F32)
        for bit, row in enumerate(rows):
            new_re, new_im = cmul(out_re, out_im, re[row : row + 1], im[row : row + 1])
            on = (exponent >> bit) & 1 == 1
            out_re = jnp.where(on, new_re, out_re)
            out_im = jnp.where(on, new_im, out_im)
        return out_re, out_im

    def one_chunk(c, _):
        lanes = pl.ds(pl.multiple_of(c * 128, 128), 128)
        f = par[1, pl.ds(c, 1), :]
        f_head = jnp.floor(f * 2048.0) * (1.0 / 2048.0)
        f_tail = f - f_head
        first = power * (f_head * TURN_HEAD)
        second = power * (f_head * TURN_TAIL + f_tail * TURN)
        turn = (first - jnp.floor(first + 0.5)) + (second - jnp.floor(second + 0.5))
        turn = turn - jnp.floor(turn + 0.5)
        square = turn * turn
        sine = turn * horner(SINE, square)
        cosine = horner(COSINE, square)
        size = jnp.exp(-power * par[0, pl.ds(c, 1), :])
        re = size * (1.0 - 2.0 * sine * sine)
        im = size * (2.0 * sine * cosine)
        g_re, g_im = par[2, pl.ds(c, 1), :], par[3, pl.ds(c, 1), :]
        l_re, l_im = cmul(g_re, g_im, re[0:1], im[0:1])
        empty = jnp.zeros((3, 128), F32)
        for single, v, g, lead in ((row_re, re, g_re, l_re), (row_im, im, g_im, l_im)):
            single[:, lanes] = jnp.concatenate(
                [v[7:8], v[10:11], v[13:14], g, lead, empty], axis=0
            )
        block_re[:, lanes], block_im[:, lanes] = choose(place8, (7, 8, 9), re, im)
        w_re, w_im = choose(ahead_z, (13, 14, 15), re, im)
        wr[:, lanes] = jnp.where(ahead_z >= 0, w_re, 0.0)
        wi[:, lanes] = jnp.where(ahead_z >= 0, w_im, 0.0)
        vr[:, lanes], vi[:, lanes] = choose(ahead_x, (10, 11, 12), re, im)
        t_re, t_im = choose(place8, (0, 1, 2), re, im)
        for row in range(3, 7):
            n_re, n_im = cmul(t_re, t_im, re[row : row + 1], im[row : row + 1])
            t_re = jnp.concatenate([t_re, n_re], axis=0)
            t_im = jnp.concatenate([t_im, n_im], axis=0)
        pr_head[:, lanes], pr_tail[:, lanes] = halves(t_re)
        pi_head[:, lanes], pi_tail[:, lanes] = halves(t_im)
        return 0

    lax.fori_loop(0, WIDE // 128, one_chunk, 0, unroll=4)

    for j in range(WIDE // FILT):
        lanes = slice(FILT * j, FILT * j + FILT)
        both_head, both_tail = halves(jnp.concatenate([row_re[:, lanes], row_im[:, lanes]], axis=0))
        full = dot3(both_head, both_tail, *lead_tables(lanes, pr_head, pr_tail, pi_head, pi_tail), 1)
        full_re = full[0:8, 0:128] - full[8:16, 128:256]
        full_im = full[0:8, 128:256] + full[8:16, 0:128]
        response[j : j + 1, :] = full_re[ROW_GAIN : ROW_GAIN + 1]
        response[8 + j : 9 + j, :] = full_im[ROW_GAIN : ROW_GAIN + 1]


def delayed(row):
    lag = lax.broadcasted_iota(jnp.int32, (128, 128), 1) - lax.broadcasted_iota(
        jnp.int32, (128, 128), 0
    )
    rolled = pltpu.roll(jnp.broadcast_to(row, (128, 128)), 0, 1, stride=1, stride_axis=0)
    return jnp.where(lag >= 0, rolled, 0.0)


def column_kernel(
    place, x, flip, pr_head, pr_tail, pi_head, pi_tail, row_re, row_im, wr, wi, vr, vi,
    own_core, other_core, next1, next2, next3, turned, lhs, total,
):
    zi, xc = place[0], place[1]
    shard_of = lax.broadcasted_iota(jnp.int32, (8, 256), 0) >> 2
    upper = lax.broadcasted_iota(jnp.int32, (8, 256), 0) < 4
    x_at, core = xc >> 1, xc & 1

    def over_shards(v):
        return v + pltpu.roll(v, 4, 0)

    def arrange(group):
        base = 128 * group
        rows = x[64 * group : 64 * group + 64, :]
        turned[base : base + 128, :] = dot(jnp.concatenate(halves(rows), axis=0), flip[...])
        for pair in range(4):
            columns = [
                jnp.concatenate(
                    [
                        turned[pl.ds(base + 64 * h + 7 - q, 8, stride=8), :]
                        for q in (2 * pair, 2 * pair + 1)
                    ],
                    axis=0,
                ).astype(BF16)
                for h in (0, 1, 0)
            ]
            at = 64 * group + 16 * pair
            lhs[at : at + 16, :] = jnp.concatenate(columns, axis=1)

    def of_group(group, lanes):
        e_re, e_im = (
            dot(
                lhs[64 * group : 64 * group + 64, :],
                jnp.concatenate([head[:, lanes], head[:, lanes], tail[:, lanes]], axis=0),
            )
            for head, tail in ((pr_head, pr_tail), (pi_head, pi_tail))
        )
        step_re = row_re[ROW_128 : ROW_128 + 1, lanes]
        step_im = row_im[ROW_128 : ROW_128 + 1, lanes]
        s_re, s_im = e_re[56:64], e_im[56:64]
        for q in range(6, -1, -1):
            s_re, s_im = cmul(s_re, s_im, step_re, step_im)
            s_re = s_re + e_re[8 * q : 8 * q + 8]
            s_im = s_im + e_im[8 * q : 8 * q + 8]
        rows = slice(8 * group, 8 * group + 8)
        weighted = cmul(s_re, s_im, wr[rows, lanes], wi[rows, lanes])
        own = [jnp.where(shard_of == zi - 2 * group, v, 0.0) for v in (s_re, s_im)]
        return [over_shards(v) for v in (*weighted, *own)]

    parts = [slice(256 * part, 256 * part + 256) for part in range(WIDE // 256)]
    arrange(0)
    for lanes in parts:
        for k, v in enumerate(of_group(0, lanes)):
            total[k, :, lanes] = v

    for group in range(1, 4):

        @pl.when(zi >= 2 * group)
        def _(group=group):
            arrange(group)
            for lanes in parts:
                for k, v in enumerate(of_group(group, lanes)):
                    total[k, :, lanes] = total[k, :, lanes] + v

    for lanes in parts:
        b_re, b_im, o_re, o_im = (total[k, :, lanes] for k in range(4))
        i_re, i_im = cmul(
            b_re, b_im,
            row_re[ROW_8192 : ROW_8192 + 1, lanes], row_im[ROW_8192 : ROW_8192 + 1, lanes],
        )
        before = jnp.where(upper, b_re, b_im)
        through = jnp.where(upper, i_re + o_re, i_im + o_im)
        for row, sent in enumerate((own_core, next1, next2, next3, other_core)):
            if row == 0:
                state = before
            elif row == 4:
                state = jnp.where(core == 0, through, before)
            else:
                state = jnp.where(x_at + row < 4, through, before)
            turn = vi[row : row + 1, lanes]
            sent[:, lanes] = state * vr[row : row + 1, lanes] + pltpu.roll(
                state, 4, 0
            ) * jnp.where(upper, -turn, turn)

    shard = jnp.where(xc == 0, zi + 1, zi)
    inside = shard < 8
    row = jnp.minimum(shard, 7) * 32
    halo = jnp.concatenate(
        [x[pl.ds(row + 8 * d, 1), :] for d in range(4)] + [jnp.zeros((4, 128), F32)],
        axis=0,
    )
    halo = jnp.where(inside, halo, 0.0)
    nothing = jnp.zeros((8, 128), F32)
    for sent, v in ((own_core, nothing), (next1, nothing), (next2, nothing), (next3, halo), (other_core, halo)):
        sent[:, WIDE : WIDE + 128] = v


def local_kernel(
    place, x, flip, pr_head, pr_tail, pi_head, pi_tail, row_re, row_im, block_re, block_im, response,
    local,
):
    zi = place[0]
    n_head, n_tail = halves(x[pl.ds(pl.multiple_of(32 * zi, 32), 32), :])
    x_head, x_tail = (dot(v, flip[...]).astype(BF16) for v in (n_head, n_tail))
    row8 = lax.broadcasted_iota(jnp.int32, (8, FILT), 0)
    for j in range(WIDE // FILT):
        lanes = slice(FILT * j, FILT * j + FILT)
        l_re = dot3(x_head, x_tail, pr_head[:, lanes], pr_tail[:, lanes])
        l_im = dot3(x_head, x_tail, pi_head[:, lanes], pi_tail[:, lanes])
        g_re, g_im = (v[ROW_LEAD : ROW_LEAD + 1, lanes] for v in (row_re, row_im))
        s_re, s_im, end_re, end_im = [], [], [], []
        for d in range(4):
            q_re, q_im = cmul(l_re[8 * d : 8 * d + 8], l_im[8 * d : 8 * d + 8], g_re, g_im)
            for step in (1, 2, 4):
                t_re, t_im = cmul(
                    pltpu.roll(q_re, step, 0), pltpu.roll(q_im, step, 0),
                    block_re[step : step + 1, lanes], block_im[step : step + 1, lanes],
                )
                q_re = q_re + jnp.where(row8 >= step, t_re, 0.0)
                q_im = q_im + jnp.where(row8 >= step, t_im, 0.0)
            s_re.append(jnp.where(row8 >= 1, pltpu.roll(q_re, 1, 0), 0.0))
            s_im.append(jnp.where(row8 >= 1, pltpu.roll(q_im, 1, 0), 0.0))
            end_re.append(q_re[7:8])
            end_im.append(q_im[7:8])
        none = [jnp.zeros((4, FILT), F32)]
        full = dot3(
            *halves(jnp.concatenate(s_re + end_re + none + s_im + end_im + none, axis=0)),
            *lead_tables(lanes, pr_head, pr_tail, pi_head, pi_tail), 1,
        )
        matrices = [delayed(response[row : row + 1, :]) for row in (j, 8 + j)]
        own = dot3(n_head, n_tail, *halves(jnp.concatenate(matrices, axis=1)))
        f_re = full[0:40, 0:128] - full[40:80, 128:256]
        f_im = full[0:40, 128:256] + full[40:80, 0:128]
        local[j, 0, 0:32, :], local[j, 0, 32:40, :] = f_re[0:32] + own[:, 0:128], f_re[32:40]
        local[j, 1, 0:32, :], local[j, 1, 32:40, :] = f_im[0:32] + own[:, 128:256], f_im[32:40]


def peak_kernel(
    place, delay, antenna, own_core, other_core, own_sum, other_sum, local, response,
    pr_head, pr_tail, pi_head, pi_tail, row_re, row_im, block_re, block_im,
    out, grouped, shifted,
):
    zi, xc = place[0], place[1]
    keep = jnp.where(jnp.logical_and(zi == 7, xc == 7), 0.0, 1.0)
    ahead_lanes = slice(WIDE, WIDE + 128)
    second = (xc & 1) == 1
    halo = jnp.where(second, other_sum[:, ahead_lanes], other_core[:, ahead_lanes])
    h_head, h_tail = halves(response[...])
    bottom = lax.broadcasted_iota(jnp.int32, (8, 128), 0) == 7

    for j in range(WIDE // FILT):
        lanes = slice(FILT * j, FILT * j + FILT)
        single = [
            v[row : row + 1, lanes] for row in (ROW_LEAD, ROW_1024) for v in (row_re, row_im)
        ]
        q = own_sum[:, lanes] + other_sum[:, lanes]
        q_re, q_im = cmul(
            q, pltpu.roll(q, 4, 0),
            jnp.where(second, single[2], 1.0), jnp.where(second, single[3], 0.0),
        )
        q = own_core[:, lanes] + other_core[:, lanes]
        q_re, q_im = cmul(q_re + q, q_im + pltpu.roll(q, 4, 0), *single[:2])
        states = [
            cmul(
                jnp.broadcast_to(q_re[d : d + 1], (8, FILT)),
                jnp.broadcast_to(q_im[d : d + 1], (8, FILT)),
                block_re[:, lanes], block_im[:, lanes],
            )
            for d in range(4)
        ]
        s_re, s_im = zip(*states, cmul(q_re, q_im, *single[2:]))
        full = dot3(
            *halves(jnp.concatenate(s_re + s_im, axis=0)),
            *lead_tables(lanes, pr_head, pr_tail, pi_head, pi_tail), 1,
        )
        f_re = full[0:40, 0:128] - full[40:80, 128:256] + local[j, 0]
        f_im = full[0:40, 128:256] + full[40:80, 0:128] + local[j, 1]
        for c, f in enumerate((f_re, f_im)):
            after = f[32:40] * keep
            for d in range(4):
                own = f[8 * d : 8 * d + 8]
                grouped[c, d, 8 * j : 8 * j + 8, :] = own
                grouped[c, d, 64 + 8 * j : 72 + 8 * j, :] = jnp.where(
                    bottom, after[d : d + 1], pltpu.roll(own, 7, 0)
                )

    for d in range(4):
        ahead = dot3(h_head, h_tail, *halves(delayed(halo[d : d + 1])))
        for c in range(2):
            rows = pl.ds(71, 8, stride=8)
            grouped[c, d, rows, :] = grouped[c, d, rows, :] + ahead[8 * c : 8 * c + 8]

    early = lax.broadcasted_iota(jnp.int32, (64, 128), 1) < 64
    for c in range(2):
        for d in range(4):
            t = grouped[c, d, 0:128, :].T
            top, low = t[0:64], t[64:128]
            shifted[c, d, 0:64, :] = jnp.where(early, top, pltpu.roll(low, 64, 1))
            shifted[c, d, 64:128, :] = jnp.where(early, low, top)
            shifted[c, d, 128:192, :] = jnp.where(early, pltpu.roll(top, 64, 1), low)

    def one_sky(s, best):
        total = [None] * 4
        for d in range(4):
            rows = pl.ds(delay[d, s], 64)
            for c in range(2):
                piece = shifted[c, d, rows, :]
                for p in range(2 if d else 1):
                    term = antenna[4 * p + d, s] * piece
                    k = 2 * p + c
                    total[k] = term if total[k] is None else total[k] + term
        energy = (total[0] * total[0] + total[1] * total[1]) + (
            total[2] * total[2] + total[3] * total[3]
        )
        return jnp.maximum(best, energy)

    best = lax.fori_loop(0, SKY, one_sky, jnp.zeros((64, 128), F32), unroll=4)
    turned = best.T
    for j in range(8):
        for m in range(8):
            row = 8 * j + m
            out[j : j + 1, 128 * m : 128 * m + 128] = jnp.concatenate(
                [turned[row : row + 1], turned[64 + row : 65 + row]], axis=1
            )


def call(kernel, n_scalar, n_vector, shapes, scratch):
    scalar, vector = (pl.BlockSpec(memory_space=m) for m in (pltpu.SMEM, pltpu.VMEM))
    return pl.pallas_call(
        kernel,
        out_shape=[jax.ShapeDtypeStruct(*s) for s in shapes],
        in_specs=[scalar] * n_scalar + [vector] * n_vector,
        out_specs=[vector] * len(shapes),
        scratch_shapes=[pltpu.VMEM(*s) for s in scratch],
        compiler_params=pltpu.CompilerParams(vmem_limit_bytes=VMEM_LIMIT),
    )


TABLE, EIGHT = ((128, WIDE), BF16), ((8, WIDE), F32)
PREPARED = [TABLE] * 4 + [EIGHT] * 4 + [((32, WIDE), F32)] * 2 + [EIGHT] * 2
PREPARED += [((16, 128), F32), ((8, SKY), F32), ((4, SKY), jnp.int32)]
STATE = ((8, WIDE + 128), F32)


def prepare(*args):
    return call(prepare_kernel, 1, 6, PREPARED, [((4, 16, 128), F32)])(*args)


def of_column(*args):
    scratch = [((520, 128), F32), ((256, 384), BF16), ((4, 8, WIDE), F32)]
    return call(column_kernel, 1, 12, [STATE] * 5, scratch)(*args)


def of_device(*args):
    return call(local_kernel, 1, 11, [((8, 2, 40, 128), F32)], [])(*args)[0]


def to_peak(*args):
    scratch = [((2, 4, 136, 128), F32), ((2, 4, 192, 128), F32)]
    return call(peak_kernel, 3, 14, [((8, 1024), F32)], scratch)(*args)[0]


def shards(strain, decay_rate, frequency, gain, member, sky_delay, antenna):
    sent = jnp.broadcast_to(strain.reshape(1, 8, 128), (32, 8, 128))
    column = lax.all_to_all(sent, ("z", "det"), 0, 0, tiled=True).reshape(256, 128)
    plane = 2 * lax.axis_index("x") + lax.axis_index("core")
    place = jnp.stack([lax.axis_index("z"), plane, lax.axis_index("det")]).astype(jnp.int32)
    flip = jnp.asarray(np.eye(128, dtype=np.float32)[::-1], dtype=BF16)
    *tables, rr, ri, br, bi, wr, wi, vr, vi, response, weight, delay = prepare(
        place, decay_rate.reshape(64, 128), frequency.reshape(64, 128), gain, member.reshape(64, 128),
        jnp.transpose(antenna, (1, 2, 0)).reshape(8, SKY), sky_delay.T,
    )
    own_core, other_core, *following = of_column(
        place, column, flip, *tables, rr, ri, wr, wi, vr, vi
    )
    got = [
        lax.ppermute(v, "x", [(x, (x + k) % 4) for x in range(4)])
        for k, v in enumerate(following, 1)
    ]
    local = of_device(place, column, flip, *tables, rr, ri, br, bi, response)
    *got, local = lax.optimization_barrier((*got, local))
    own_sum = got[0] + got[1] + got[2]
    swap = [(0, 1), (1, 0)]
    return to_peak(
        place, delay, weight, own_core, lax.ppermute(other_core, "core", swap),
        own_sum, lax.ppermute(own_sum, "core", swap), local, response, *tables, rr, ri, br, bi,
    )


def solution(mesh):
    fine = Mesh(mesh.devices.reshape(8, 4, 2, 4), ("z", "x", "core", "det"))
    time = ("z", "x", "core")
    in_specs = (P("det", time), P(), P(), P(), P(), P(), P())
    return jax.shard_map(
        shards, mesh=fine, in_specs=in_specs, out_specs=P("det", time), check_vma=False
    )
```

```python
import math

import jax
import jax.numpy as jnp
import numpy as np
from jax import lax
from jax.experimental import pallas as pl
from jax.experimental.pallas import tpu as pltpu
from jax.sharding import Mesh, PartitionSpec as P

FILT = 256
SKY = 64
WIDE = 8 * FILT
F32, BF16 = jnp.float32, jnp.bfloat16

TURN = 1.0 / (2.0 * math.pi)
TURN_HEAD = math.floor(TURN * 2**14) / 2**14
TURN_TAIL = TURN - TURN_HEAD

ROW_128, ROW_1024, ROW_8192, ROW_GAIN, ROW_LEAD = 0, 1, 2, 3, 4

VMEM_LIMIT = 16 * 2**20


def taylor(first, start, count):
    return [
        first * (-1) ** k * math.pi ** (2 * k + start) / math.factorial(2 * k + start)
        for k in range(count)
    ]


SINE, COSINE = taylor(1.0, 1, 8), taylor(1.0, 0, 9)


def horner(coefficients, square):
    total = jnp.full(square.shape, coefficients[-1], F32)
    for c in coefficients[-2::-1]:
        total = total * square + c
    return total


def cmul(ar, ai, br, bi):
    return ar * br - ai * bi, ar * bi + ai * br


def halves(x):
    head = x.astype(BF16)
    return head, (x - head.astype(F32)).astype(BF16)


def dot(a, b, contract_b=0):
    return lax.dot_general(
        a, b, (((1,), (contract_b,)), ((), ())), preferred_element_type=F32
    )


def dot3(a_head, a_tail, b_head, b_tail, contract_b=0):
    rows = a_head.shape[0]
    both = dot(jnp.concatenate([a_head, a_tail], axis=0), b_head, contract_b)
    return both[:rows] + both[rows:] + dot(a_head, b_tail, contract_b)


def lead_tables(lanes, pr_head, pr_tail, pi_head, pi_tail):
    return (
        jnp.concatenate([pr_head[:, lanes], pi_head[:, lanes]], axis=0),
        jnp.concatenate([pr_tail[:, lanes], pi_tail[:, lanes]], axis=0),
    )


def prepare_kernel(
    place, decay, frequency, gain, member, antenna, sky_delay,
    pr_head, pr_tail, pi_head, pi_tail, row_re, row_im, block_re, block_im, wr, wi, vr, vi, response,
    weight, delay, par,
):
    zi, xc, det = place[0], place[1], place[2]

    delay[...] = sky_delay[...]
    one, two = antenna[0:4, :], antenna[4:8, :]
    scale = jnp.maximum(jnp.abs(one[0:1]), jnp.abs(two[0:1]))
    divisor = jnp.where(scale > 0.0, scale, 1.0)
    a, b = jnp.where(scale > 0.0, one[0:1] / divisor, 1.0), two[0:1] / divisor
    size = jnp.sqrt(a * a + b * b)
    cosine, sine = a / size, b / size
    weight[...] = jnp.concatenate([cosine * one + sine * two, cosine * two - sine * one], axis=0)

    index = [
        member[pl.ds(pl.multiple_of(16 * det + 8 * half, 8), 8), :] for half in range(2)
    ]
    high, low = [v >> 7 for v in index], [v & 127 for v in index]

    def one_row(r, carried):
        lanes = pl.ds(pl.multiple_of(r * 128, 128), 128)
        values = (
            decay[pl.ds(r, 1), :],
            frequency[pl.ds(r, 1), :],
            gain[0:1, lanes],
            gain[1:2, lanes],
        )
        spread = [jnp.broadcast_to(v, (8, 128)) for v in values]
        return tuple(
            jnp.where(
                high[h] == r,
                jnp.take_along_axis(spread[k], low[h], axis=1),
                carried[4 * h + k],
            )
            for h in range(2)
            for k in range(4)
        )

    nothing = jnp.zeros((8, 128), F32)
    found = lax.fori_loop(0, 64, one_row, (nothing,) * 8, unroll=8)
    for h in range(2):
        for k in range(4):
            par[k, 8 * h : 8 * h + 8, :] = found[4 * h + k]

    power = jnp.left_shift(1, lax.broadcasted_iota(jnp.int32, (16, 128), 0)).astype(F32)
    place8 = lax.broadcasted_iota(jnp.int32, (8, 128), 0)
    ahead_z = zi - 1 - (lax.broadcasted_iota(jnp.int32, (32, 128), 0) >> 2)
    core = xc & 1
    ahead_x = jnp.where(place8 == 4, 6 * core, jnp.where(place8 == 0, 7, (2 * place8 - 1 - core) & 7))

    def choose(exponent, rows, re, im):
        out_re = jnp.ones(exponent.shape, F32)
        out_im = jnp.zeros(exponent.shape, F32)
        for bit, row in enumerate(rows):
            new_re, new_im = cmul(out_re, out_im, re[row : row + 1], im[row : row + 1])
            on = (exponent >> bit) & 1 == 1
            out_re = jnp.where(on, new_re, out_re)
            out_im = jnp.where(on, new_im, out_im)
        return out_re, out_im

    def one_chunk(c, _):
        lanes = pl.ds(pl.multiple_of(c * 128, 128), 128)
        f = par[1, pl.ds(c, 1), :]
        f_head = jnp.floor(f * 2048.0) * (1.0 / 2048.0)
        f_tail = f - f_head
        first = power * (f_head * TURN_HEAD)
        second = power * (f_head * TURN_TAIL + f_tail * TURN)
        turn = (first - jnp.floor(first + 0.5)) + (second - jnp.floor(second + 0.5))
        turn = turn - jnp.floor(turn + 0.5)
        square = turn * turn
        sine = turn * horner(SINE, square)
        cosine = horner(COSINE, square)
        size = jnp.exp(-power * par[0, pl.ds(c, 1), :])
        re = size * (1.0 - 2.0 * sine * sine)
        im = size * (2.0 * sine * cosine)
        g_re, g_im = par[2, pl.ds(c, 1), :], par[3, pl.ds(c, 1), :]
        l_re, l_im = cmul(g_re, g_im, re[0:1], im[0:1])
        empty = jnp.zeros((3, 128), F32)
        for single, v, g, lead in ((row_re, re, g_re, l_re), (row_im, im, g_im, l_im)):
            single[:, lanes] = jnp.concatenate(
                [v[7:8], v[10:11], v[13:14], g, lead, empty], axis=0
            )
        block_re[:, lanes], block_im[:, lanes] = choose(place8, (7, 8, 9), re, im)
        w_re, w_im = choose(ahead_z, (13, 14, 15), re, im)
        wr[:, lanes] = jnp.where(ahead_z >= 0, w_re, 0.0)
        wi[:, lanes] = jnp.where(ahead_z >= 0, w_im, 0.0)
        vr[:, lanes], vi[:, lanes] = choose(ahead_x, (10, 11, 12), re, im)
        t_re, t_im = choose(place8, (0, 1, 2), re, im)
        for row in range(3, 7):
            n_re, n_im = cmul(t_re, t_im, re[row : row + 1], im[row : row + 1])
            t_re = jnp.concatenate([t_re, n_re], axis=0)
            t_im = jnp.concatenate([t_im, n_im], axis=0)
        pr_head[:, lanes], pr_tail[:, lanes] = halves(t_re)
        pi_head[:, lanes], pi_tail[:, lanes] = halves(t_im)
        return 0

    lax.fori_loop(0, WIDE // 128, one_chunk, 0, unroll=4)

    for j in range(WIDE // FILT):
        lanes = slice(FILT * j, FILT * j + FILT)
        both_head, both_tail = halves(jnp.concatenate([row_re[:, lanes], row_im[:, lanes]], axis=0))
        full = dot3(both_head, both_tail, *lead_tables(lanes, pr_head, pr_tail, pi_head, pi_tail), 1)
        full_re = full[0:8, 0:128] - full[8:16, 128:256]
        full_im = full[0:8, 128:256] + full[8:16, 0:128]
        response[j : j + 1, :] = full_re[ROW_GAIN : ROW_GAIN + 1]
        response[8 + j : 9 + j, :] = full_im[ROW_GAIN : ROW_GAIN + 1]


def delayed(row):
    lag = lax.broadcasted_iota(jnp.int32, (128, 128), 1) - lax.broadcasted_iota(
        jnp.int32, (128, 128), 0
    )
    rolled = pltpu.roll(jnp.broadcast_to(row, (128, 128)), 0, 1, stride=1, stride_axis=0)
    return jnp.where(lag >= 0, rolled, 0.0)


def column_kernel(
    place, x, flip, pr_head, pr_tail, pi_head, pi_tail, row_re, row_im, wr, wi, vr, vi,
    own_core, other_core, next1, next2, next3, turned, lhs, total,
):
    zi, xc = place[0], place[1]
    sizes, starts = (8, 24), (0, 8)
    upper = lax.broadcasted_iota(jnp.int32, (8, 256), 0) < 4
    x_at, core = xc >> 1, xc & 1

    def shard_of(size):
        return lax.broadcasted_iota(jnp.int32, (size, 256), 0) >> 2

    def over_shards(v):
        v = sum(v[at : at + 8] for at in range(0, v.shape[0], 8))
        return v + pltpu.roll(v, 4, 0)

    def arrange(group):
        size, start = sizes[group], starts[group]
        base = 16 * start
        rows = x[8 * start : 8 * (start + size), :]
        turned[base : base + 16 * size, :] = dot(jnp.concatenate(halves(rows), axis=0), flip[...])
        for pair in range(4):
            columns = [
                jnp.concatenate(
                    [
                        turned[pl.ds(base + 8 * size * h + 7 - q, size, stride=8), :]
                        for q in (2 * pair, 2 * pair + 1)
                    ],
                    axis=0,
                ).astype(BF16)
                for h in (0, 1, 0)
            ]
            at = 8 * start + 2 * size * pair
            lhs[at : at + 2 * size, :] = jnp.concatenate(columns, axis=1)

    def of_group(group, lanes):
        size, start = sizes[group], starts[group]
        e_re, e_im = (
            dot(
                lhs[8 * start : 8 * (start + size), :],
                jnp.concatenate([head[:, lanes], head[:, lanes], tail[:, lanes]], axis=0),
            )
            for head, tail in ((pr_head, pr_tail), (pi_head, pi_tail))
        )
        step_re = row_re[ROW_128 : ROW_128 + 1, lanes]
        step_im = row_im[ROW_128 : ROW_128 + 1, lanes]
        s_re, s_im = e_re[7 * size :], e_im[7 * size :]
        for q in range(6, -1, -1):
            s_re, s_im = cmul(s_re, s_im, step_re, step_im)
            s_re = s_re + e_re[size * q : size * q + size]
            s_im = s_im + e_im[size * q : size * q + size]
        rows = slice(start, start + size)
        weighted = cmul(s_re, s_im, wr[rows, lanes], wi[rows, lanes])
        own = [jnp.where(shard_of(size) == zi - start // 4, v, 0.0) for v in (s_re, s_im)]
        return [over_shards(v) for v in (*weighted, *own)]

    parts = [slice(256 * part, 256 * part + 256) for part in range(WIDE // 256)]
    arrange(0)
    for lanes in parts:
        for k, v in enumerate(of_group(0, lanes)):
            total[k, :, lanes] = v

    @pl.when(zi >= 2)
    def _():
        arrange(1)
        for lanes in parts:
            for k, v in enumerate(of_group(1, lanes)):
                total[k, :, lanes] = total[k, :, lanes] + v

    for lanes in parts:
        b_re, b_im, o_re, o_im = (total[k, :, lanes] for k in range(4))
        i_re, i_im = cmul(
            b_re, b_im,
            row_re[ROW_8192 : ROW_8192 + 1, lanes], row_im[ROW_8192 : ROW_8192 + 1, lanes],
        )
        before = jnp.where(upper, b_re, b_im)
        through = jnp.where(upper, i_re + o_re, i_im + o_im)
        for row, sent in enumerate((own_core, next1, next2, next3, other_core)):
            if row == 0:
                state = before
            elif row == 4:
                state = jnp.where(core == 0, through, before)
            else:
                state = jnp.where(x_at + row < 4, through, before)
            turn = vi[row : row + 1, lanes]
            sent[:, lanes] = state * vr[row : row + 1, lanes] + pltpu.roll(
                state, 4, 0
            ) * jnp.where(upper, -turn, turn)

    shard = jnp.where(xc == 0, zi + 1, zi)
    inside = shard < 8
    row = jnp.minimum(shard, 7) * 32
    halo = jnp.concatenate(
        [x[pl.ds(row + 8 * d, 1), :] for d in range(4)] + [jnp.zeros((4, 128), F32)],
        axis=0,
    )
    halo = jnp.where(inside, halo, 0.0)
    nothing = jnp.zeros((8, 128), F32)
    for sent, v in ((own_core, nothing), (next1, nothing), (next2, nothing), (next3, halo), (other_core, halo)):
        sent[:, WIDE : WIDE + 128] = v


def local_kernel(
    place, x, flip, pr_head, pr_tail, pi_head, pi_tail, row_re, row_im, block_re, block_im, response,
    local,
):
    zi = place[0]
    n_head, n_tail = halves(x[pl.ds(pl.multiple_of(32 * zi, 32), 32), :])
    x_head, x_tail = (dot(v, flip[...]).astype(BF16) for v in (n_head, n_tail))
    row8 = lax.broadcasted_iota(jnp.int32, (8, FILT), 0)
    for j in range(WIDE // FILT):
        lanes = slice(FILT * j, FILT * j + FILT)
        l_re = dot3(x_head, x_tail, pr_head[:, lanes], pr_tail[:, lanes])
        l_im = dot3(x_head, x_tail, pi_head[:, lanes], pi_tail[:, lanes])
        g_re, g_im = (v[ROW_LEAD : ROW_LEAD + 1, lanes] for v in (row_re, row_im))
        s_re, s_im, end_re, end_im = [], [], [], []
        for d in range(4):
            q_re, q_im = cmul(l_re[8 * d : 8 * d + 8], l_im[8 * d : 8 * d + 8], g_re, g_im)
            for step in (1, 2, 4):
                t_re, t_im = cmul(
                    pltpu.roll(q_re, step, 0), pltpu.roll(q_im, step, 0),
                    block_re[step : step + 1, lanes], block_im[step : step + 1, lanes],
                )
                q_re = q_re + jnp.where(row8 >= step, t_re, 0.0)
                q_im = q_im + jnp.where(row8 >= step, t_im, 0.0)
            s_re.append(jnp.where(row8 >= 1, pltpu.roll(q_re, 1, 0), 0.0))
            s_im.append(jnp.where(row8 >= 1, pltpu.roll(q_im, 1, 0), 0.0))
            end_re.append(q_re[7:8])
            end_im.append(q_im[7:8])
        none = [jnp.zeros((4, FILT), F32)]
        full = dot3(
            *halves(jnp.concatenate(s_re + end_re + none + s_im + end_im + none, axis=0)),
            *lead_tables(lanes, pr_head, pr_tail, pi_head, pi_tail), 1,
        )
        matrices = [delayed(response[row : row + 1, :]) for row in (j, 8 + j)]
        own = dot3(n_head, n_tail, *halves(jnp.concatenate(matrices, axis=1)))
        f_re = full[0:40, 0:128] - full[40:80, 128:256]
        f_im = full[0:40, 128:256] + full[40:80, 0:128]
        local[j, 0, 0:32, :], local[j, 0, 32:40, :] = f_re[0:32] + own[:, 0:128], f_re[32:40]
        local[j, 1, 0:32, :], local[j, 1, 32:40, :] = f_im[0:32] + own[:, 128:256], f_im[32:40]


def peak_kernel(
    place, delay, antenna, own_core, other_core, own_sum, other_sum, local, response,
    pr_head, pr_tail, pi_head, pi_tail, row_re, row_im, block_re, block_im,
    out, grouped, shifted,
):
    zi, xc = place[0], place[1]
    keep = jnp.where(jnp.logical_and(zi == 7, xc == 7), 0.0, 1.0)
    ahead_lanes = slice(WIDE, WIDE + 128)
    second = (xc & 1) == 1
    halo = jnp.where(second, other_sum[:, ahead_lanes], other_core[:, ahead_lanes])
    h_head, h_tail = halves(response[...])
    bottom = lax.broadcasted_iota(jnp.int32, (8, 128), 0) == 7

    for j in range(WIDE // FILT):
        lanes = slice(FILT * j, FILT * j + FILT)
        single = [
            v[row : row + 1, lanes] for row in (ROW_LEAD, ROW_1024) for v in (row_re, row_im)
        ]
        q = own_sum[:, lanes] + other_sum[:, lanes]
        q_re, q_im = cmul(
            q, pltpu.roll(q, 4, 0),
            jnp.where(second, single[2], 1.0), jnp.where(second, single[3], 0.0),
        )
        q = own_core[:, lanes] + other_core[:, lanes]
        q_re, q_im = cmul(q_re + q, q_im + pltpu.roll(q, 4, 0), *single[:2])
        states = [
            cmul(
                jnp.broadcast_to(q_re[d : d + 1], (8, FILT)),
                jnp.broadcast_to(q_im[d : d + 1], (8, FILT)),
                block_re[:, lanes], block_im[:, lanes],
            )
            for d in range(4)
        ]
        s_re, s_im = zip(*states, cmul(q_re, q_im, *single[2:]))
        full = dot3(
            *halves(jnp.concatenate(s_re + s_im, axis=0)),
            *lead_tables(lanes, pr_head, pr_tail, pi_head, pi_tail), 1,
        )
        f_re = full[0:40, 0:128] - full[40:80, 128:256] + local[j, 0]
        f_im = full[0:40, 128:256] + full[40:80, 0:128] + local[j, 1]
        for c, f in enumerate((f_re, f_im)):
            after = f[32:40] * keep
            for d in range(4):
                own = f[8 * d : 8 * d + 8]
                grouped[c, d, 8 * j : 8 * j + 8, :] = own
                grouped[c, d, 64 + 8 * j : 72 + 8 * j, :] = jnp.where(
                    bottom, after[d : d + 1], pltpu.roll(own, 7, 0)
                )

    for d in range(4):
        ahead = dot3(h_head, h_tail, *halves(delayed(halo[d : d + 1])))
        for c in range(2):
            rows = pl.ds(71, 8, stride=8)
            grouped[c, d, rows, :] = grouped[c, d, rows, :] + ahead[8 * c : 8 * c + 8]

    early = lax.broadcasted_iota(jnp.int32, (64, 128), 1) < 64
    for c in range(2):
        for d in range(4):
            t = grouped[c, d, 0:128, :].T
            top, low = t[0:64], t[64:128]
            shifted[c, d, 0:64, :] = jnp.where(early, top, pltpu.roll(low, 64, 1))
            shifted[c, d, 64:128, :] = jnp.where(early, low, top)
            shifted[c, d, 128:192, :] = jnp.where(early, pltpu.roll(top, 64, 1), low)

    def one_sky(s, best):
        total = [None] * 4
        for d in range(4):
            rows = pl.ds(delay[d, s], 64)
            for c in range(2):
                piece = shifted[c, d, rows, :]
                for p in range(2 if d else 1):
                    term = antenna[4 * p + d, s] * piece
                    k = 2 * p + c
                    total[k] = term if total[k] is None else total[k] + term
        energy = (total[0] * total[0] + total[1] * total[1]) + (
            total[2] * total[2] + total[3] * total[3]
        )
        return jnp.maximum(best, energy)

    best = lax.fori_loop(0, SKY, one_sky, jnp.zeros((64, 128), F32), unroll=4)
    turned = best.T
    for j in range(8):
        for m in range(8):
            row = 8 * j + m
            out[j : j + 1, 128 * m : 128 * m + 128] = jnp.concatenate(
                [turned[row : row + 1], turned[64 + row : 65 + row]], axis=1
            )


def call(kernel, n_scalar, n_vector, shapes, scratch):
    scalar, vector = (pl.BlockSpec(memory_space=m) for m in (pltpu.SMEM, pltpu.VMEM))
    return pl.pallas_call(
        kernel,
        out_shape=[jax.ShapeDtypeStruct(*s) for s in shapes],
        in_specs=[scalar] * n_scalar + [vector] * n_vector,
        out_specs=[vector] * len(shapes),
        scratch_shapes=[pltpu.VMEM(*s) for s in scratch],
        compiler_params=pltpu.CompilerParams(vmem_limit_bytes=VMEM_LIMIT),
    )


TABLE, EIGHT = ((128, WIDE), BF16), ((8, WIDE), F32)
PREPARED = [TABLE] * 4 + [EIGHT] * 4 + [((32, WIDE), F32)] * 2 + [EIGHT] * 2
PREPARED += [((16, 128), F32), ((8, SKY), F32), ((4, SKY), jnp.int32)]
STATE = ((8, WIDE + 128), F32)


def prepare(*args):
    return call(prepare_kernel, 1, 6, PREPARED, [((4, 16, 128), F32)])(*args)


def of_column(*args):
    scratch = [((520, 128), F32), ((256, 384), BF16), ((4, 8, WIDE), F32)]
    return call(column_kernel, 1, 12, [STATE] * 5, scratch)(*args)


def of_device(*args):
    return call(local_kernel, 1, 11, [((8, 2, 40, 128), F32)], [])(*args)[0]


def to_peak(*args):
    scratch = [((2, 4, 136, 128), F32), ((2, 4, 192, 128), F32)]
    return call(peak_kernel, 3, 14, [((8, 1024), F32)], scratch)(*args)[0]


def shards(strain, decay_rate, frequency, gain, member, sky_delay, antenna):
    sent = jnp.broadcast_to(strain.reshape(1, 8, 128), (32, 8, 128))
    column = lax.all_to_all(sent, ("z", "det"), 0, 0, tiled=True).reshape(256, 128)
    plane = 2 * lax.axis_index("x") + lax.axis_index("core")
    place = jnp.stack([lax.axis_index("z"), plane, lax.axis_index("det")]).astype(jnp.int32)
    flip = jnp.asarray(np.eye(128, dtype=np.float32)[::-1], dtype=BF16)
    *tables, rr, ri, br, bi, wr, wi, vr, vi, response, weight, delay = prepare(
        place, decay_rate.reshape(64, 128), frequency.reshape(64, 128), gain, member.reshape(64, 128),
        jnp.transpose(antenna, (1, 2, 0)).reshape(8, SKY), sky_delay.T,
    )
    own_core, other_core, *following = of_column(
        place, column, flip, *tables, rr, ri, wr, wi, vr, vi
    )
    got = [
        lax.ppermute(v, "x", [(x, (x + k) % 4) for x in range(4)])
        for k, v in enumerate(following, 1)
    ]
    local = of_device(place, column, flip, *tables, rr, ri, br, bi, response)
    *got, local = lax.optimization_barrier((*got, local))
    own_sum = got[0] + got[1] + got[2]
    swap = [(0, 1), (1, 0)]
    return to_peak(
        place, delay, weight, own_core, lax.ppermute(other_core, "core", swap),
        own_sum, lax.ppermute(own_sum, "core", swap), local, response, *tables, rr, ri, br, bi,
    )


def solution(mesh):
    fine = Mesh(mesh.devices.reshape(8, 4, 2, 4), ("z", "x", "core", "det"))
    time = ("z", "x", "core")
    in_specs = (P("det", time), P(), P(), P(), P(), P(), P())
    return jax.shard_map(
        shards, mesh=fine, in_specs=in_specs, out_specs=P("det", time), check_vma=False
    )
```
